32 devices in a mesh: groups: 2 (over y), shot: 4 (over z), dom: 2 (over x), pair: 2 (over core).
Axes of the slice: x: 2, y: 2, z: 4, core: 2. Of those that a mesh axis runs over, the one named last changes fastest.
Arguments:
- velocity: float32 [128, 8, 8, 128], P(('groups', 'shot', 'dom')), parts along dimension 0, may hold values from 0.12 to 0.36
- density: float32 [128, 8, 8, 128], P(('groups', 'shot', 'dom')), parts along dimension 0, may hold values from 1 to 2
- owner_map: int32 [128], P('groups'), parts along dimension 0, may hold values from 0 to 63, as said below
- footprint: int32 [8, 32], P(('groups', 'shot'), 'dom'), parts along dimension 0, may hold values from 0 to 63, as said below
- aperture: int32 [8], P(('groups', 'shot')), parts along dimension 0, may hold values from 4 to 8, as said below
- source_cell: int32 [8], P(('groups', 'shot')), parts along dimension 0, may hold values from 0 to 131071
- receiver_cells: int32 [8, 512], P(('groups', 'shot')), parts along dimension 0, may hold values from 0 to 131071
- wavelet: float32 [8, 16], P(('groups', 'shot')), parts along dimension 0, may hold values from -6 to 6
- traces: float32 [8, 16, 512], P(('groups', 'shot')), parts along dimension 0, may hold values from -6 to 6
- states: float32 [8, 2, 2, 64, 32, 128], P(('groups', 'shot'), 'pair', None, 'dom'), parts along dimension 0, may hold values from -6 to 6
- stored_rims: float32 [8, 16, 2, 64, 128], P(('groups', 'shot'), None, None, 'dom'), parts along dimension 0, may hold values from -6 to 6
Outputs:
- migrated: float32 [128, 8, 8, 128], P(('groups', 'shot', 'dom'), 'pair'), parts along dimension 0
The draws below stay inside these ranges and needn't reach their ends.
There are 2 independent parts, one for each index of `groups`. The reference program is written for one: setup_inputs(seed, part) draws one part's arguments, and reference() takes and returns one part's arrays. A program takes and returns all parts, laid end to end along the dimension named above; each array names one. Nothing has to cross between parts.
Inputs may be any that keep to these rules, and one draw needn't show every extreme that they name: owner_map[g] is the row of the brick tables that holds brick g; every row holds exactly one brick. The 16 entries footprint[s, d * 16 + k] name bricks whose rows lie on the owners of dom index d, exactly 4 on each shot index; within a shot all bricks differ. Shot s uses its first aperture[s] brick columns; both ends of the range are reached in every draw.
All inputs are finite; a program needn't handle non-finite values.
Results may differ from the reference program's by a relative error of at most 0.0003.
Values sent between devices are 32-bit elements; how exact they have to be, the bound alone decides.
No kernel may reach another device: no remote copies, remote signals or barrier semaphores. Data moves between devices by JAX's collectives and lax.ppermute only.
A program may use at most 64 MiB of HBM per device.

```python
import math
import jax
import jax.numpy as jnp
from jax import lax

BX = 8
BY = 8
BZ = 128
KX = 4
KY = 4
BR_DEV = 8
STEPS = 16
NREC = 512
KD = 16
CAP = 4
NXB = 8
AX = 64
AY = 32
AZ = 128
SHOTS = 4
NBT = 64


def shared_layout(key):
    placement = jax.random.permutation(jax.random.fold_in(key, 11), NBT).astype(jnp.int32)
    brick_of_row = jnp.argsort(placement, stable=True).astype(jnp.int32)
    scores = jax.random.randint(jax.random.fold_in(key, 12), (SHOTS, NXB // KX, SHOTS, BR_DEV), 0, 1048576)
    scores = scores * BR_DEV + jnp.arange(BR_DEV, dtype=jnp.int32)
    picks = jnp.argsort(scores, axis=-1, stable=True)[..., :CAP].astype(jnp.int32)
    owner_ids = jnp.arange(SHOTS, dtype=jnp.int32)[None, None, :, None]
    column_ids = jnp.arange(NXB // KX, dtype=jnp.int32)[None, :, None, None]
    table_rows = (owner_ids * (NXB // KX) + column_ids) * BR_DEV + picks
    table_rows = table_rows.reshape(SHOTS, NXB // KX, KD)
    mixing = jax.random.randint(jax.random.fold_in(key, 13), (SHOTS, NXB // KX, KD), 0, 1048576)
    mixing = mixing * KD + jnp.arange(KD, dtype=jnp.int32)
    shuffle = jnp.argsort(mixing, axis=-1, stable=True).astype(jnp.int32)
    table_rows = jnp.take_along_axis(table_rows, shuffle, axis=-1)
    prints = brick_of_row[table_rows].reshape(SHOTS, NXB * KY)
    return (placement, prints.astype(jnp.int32))


def draw_owner_map(key, part):
    placement, prints = shared_layout(key)
    return placement


def draw_footprint(key, part):
    placement, prints = shared_layout(key)
    return prints


def draw_aperture(key, part):
    key = jax.random.fold_in(key, 3)
    widest = NXB
    narrowest = NXB // 2
    chosen_sizes = jax.random.randint(jax.random.fold_in(key, 1), (SHOTS,), narrowest, widest + 1)
    chosen_shots = jax.random.permutation(jax.random.fold_in(key, 2), SHOTS)
    chosen_sizes = chosen_sizes.at[chosen_shots[0]].set(widest).at[chosen_shots[1]].set(narrowest)
    return chosen_sizes.astype(jnp.int32)


def place_ends(values, stream_key, least, top_value):
    spot = [jax.random.randint(jax.random.fold_in(stream_key, axis), (), 0, length) for axis, length in enumerate(values.shape)]
    longest = values.shape.index(max(values.shape))
    beside = spot[:longest] + [(spot[longest] + 1) % values.shape[longest]] + spot[longest + 1:]
    return values.at[tuple(spot)].set(least).at[tuple(beside)].set(top_value)


def steps_of(key, extent, split, smallest, top_value):
    level, own = 1.0, jax.random.fold_in(key, 6)
    for dim, shards_of in split:
        draws = jnp.exp(jax.random.uniform(jax.random.fold_in(own, dim), (shards_of,), jnp.float32, smallest / len(split), top_value / len(split)))
        level = level * jnp.repeat(draws, extent[dim] // shards_of).reshape([-1 if axis == dim else 1 for axis in range(len(extent))])
    return level


def gaussian(rng, shape, width, most, split=(), kind=jnp.bfloat16):
    entries = width * jax.random.normal(rng, shape, jnp.float32)
    if split:
        entries = entries * steps_of(rng, shape, split, -0.22, 0.18)
    return jnp.clip(entries, -most, most).astype(kind)


def setup_inputs(seed: int = 0, part: int = 0) -> dict:
    key_list = jax.random.split(jax.random.key(seed), 12)
    own_keys = jax.random.split(jax.random.fold_in(key_list[11], part), 12)
    return {
        "velocity": jnp.clip(jnp.exp(math.log(0.36) - 1.09861235 * jax.random.uniform(own_keys[0], (NBT, BX, BY, BZ), jnp.float32) ** steps_of(own_keys[0], (NBT, BX, BY, BZ), ((0, 8),), -0.2, 0.2)), 0.12, 0.36),
        "density": jnp.clip(jnp.exp(math.log(2.0) - 0.6931472 * jax.random.uniform(own_keys[1], (NBT, BX, BY, BZ), jnp.float32) ** steps_of(own_keys[1], (NBT, BX, BY, BZ), ((0, 8),), -0.2, 0.2)), 1.0, 2.0),
        "owner_map": draw_owner_map(jax.random.fold_in(jax.random.fold_in(key_list[11], part), 71), part),
        "footprint": draw_footprint(jax.random.fold_in(jax.random.fold_in(key_list[11], part), 71), part),
        "aperture": draw_aperture(jax.random.fold_in(jax.random.fold_in(key_list[11], part), 71), part),
        "source_cell": place_ends(jax.random.randint(own_keys[5], (SHOTS,), 0, NXB // 2 * BX * AY * AZ), jax.random.fold_in(own_keys[5], 1), 0, (NXB // 2 * BX * AY * AZ) - 1).astype(jnp.int32),
        "receiver_cells": place_ends(jax.random.randint(own_keys[6], (SHOTS, NREC), 0, NXB // 2 * BX * AY * AZ), jax.random.fold_in(own_keys[6], 1), 0, (NXB // 2 * BX * AY * AZ) - 1).astype(jnp.int32),
        "wavelet": gaussian(own_keys[7], (SHOTS, STEPS), 1.0, 6.0, ((0, 4),), jnp.float32),
        "traces": gaussian(own_keys[8], (SHOTS, STEPS, NREC), 1.0, 6.0, ((0, 4),), jnp.float32),
        "states": gaussian(own_keys[9], (SHOTS, 2, 2, AX, AY, AZ), 1.0, 6.0, ((0, 4), (1, 2), (3, 2)), jnp.float32),
        "stored_rims": gaussian(own_keys[10], (SHOTS, STEPS, 2, AX, AZ), 1.0, 6.0, ((0, 4), (3, 2)), jnp.float32),
    }


first_weights = (0.8, -0.2, 4.0 / 105.0, -1.0 / 280.0)
second_weights = (-205.0 / 72.0, 1.6, -0.2, 8.0 / 315.0, -1.0 / 560.0)


def derivatives(padded):
    size_x = padded.shape[0] - 8
    size_y = padded.shape[1] - 8
    size_z = padded.shape[2] - 8

    def window(direction, reach):
        start = [4, 4, 4]
        start[direction] = start[direction] + reach
        return padded[start[0]:start[0] + size_x, start[1]:start[1] + size_y, start[2]:start[2] + size_z]

    centre = window(0, 0)
    laplace = (3.0 * second_weights[0]) * centre
    slopes = []
    for direction in range(3):
        slope = jnp.zeros_like(centre)
        for reach in range(1, 5):
            ahead = window(direction, reach)
            behind = window(direction, -reach)
            laplace = laplace + second_weights[reach] * (ahead + behind)
            slope = slope + first_weights[reach - 1] * (ahead - behind)
        slopes.append(slope)
    return laplace, slopes


def advance(padded, earlier, courant_sq, bends):
    laplace, slopes = derivatives(padded)
    drift = bends[0] * slopes[0] + bends[1] * slopes[1] + bends[2] * slopes[2]
    return 2.0 * padded[4:-4, 4:-4, 4:-4] - earlier + courant_sq * (laplace - drift)


def to_grid(bricks):
    blocks = bricks.reshape(NXB, KY, BX, BY, BZ).transpose(0, 2, 1, 3, 4)
    return blocks.reshape(NXB * BX, KY * BY, BZ)


def to_bricks(grid):
    blocks = grid.reshape(NXB, BX, KY, BY, BZ).transpose(0, 2, 1, 3, 4)
    return blocks.reshape(NXB * KY, BX, BY, BZ)


def reference(velocity, density, owner_map, footprint, aperture, source_cell, receiver_cells, wavelet, traces, states, stored_rims):
    def one_shot(totals, inputs):
        prints, aperture_s, source_at, receivers, pulses, recorded, fields, rim_table = inputs
        table_rows = owner_map[prints]
        columns_x = (jnp.arange(NXB * BX, dtype=jnp.int32) // BX).astype(jnp.int32)
        in_aperture = (columns_x < aperture_s)[:, None, None]
        courant = to_grid(velocity[table_rows])
        dens_grid = to_grid(density[table_rows])
        courant_sq = jnp.where(in_aperture, courant * courant, 0.0)
        log_dens = jnp.where(in_aperture, jnp.log(jnp.where(in_aperture, dens_grid, 1.0)), 0.0)
        unused, bends = derivatives(jnp.pad(log_dens, 4))
        shape = (AX, AY, AZ)

        def advance_one(moment, carry):
            src_a, src_b, rec_a, rec_b, imaged = carry
            new_src = advance(jnp.pad(src_b, 4), src_a, courant_sq, bends)
            pulse_now = lax.dynamic_index_in_dim(pulses, moment, 0, keepdims=False)
            new_src = new_src.reshape(-1).at[source_at].add(-pulse_now).reshape(shape)
            rim_now = lax.dynamic_index_in_dim(rim_table, moment, 0, keepdims=False)
            new_src = new_src.at[:, 0, :].set(rim_now[0]).at[:, AY - 1, :].set(rim_now[1])
            new_src = jnp.where(in_aperture, new_src, 0.0)
            new_rec = advance(jnp.pad(rec_b, 4), rec_a, courant_sq, bends)
            trace_now = lax.dynamic_index_in_dim(recorded, moment, 0, keepdims=False)
            new_rec = new_rec.reshape(-1).at[receivers].add(trace_now).reshape(shape)
            new_rec = jnp.where(in_aperture, new_rec, 0.0)
            imaged = imaged + new_src * new_rec
            return (src_b, new_src, rec_b, new_rec, imaged)

        start = (fields[0, 0], fields[0, 1], fields[1, 0], fields[1, 1], jnp.zeros(shape, jnp.float32))
        finish = lax.fori_loop(0, STEPS, advance_one, start)
        partial_image = to_bricks(finish[4])
        return totals.at[table_rows].add(partial_image), None

    totals = jnp.zeros((NBT, BX, BY, BZ), jnp.float32)
    totals, unused = lax.scan(one_shot, totals, (footprint, aperture, source_cell, receiver_cells, wavelet, traces, states, stored_rims))
    return totals
```

```python
import functools

import jax
import jax.numpy as jnp
import numpy as np
from jax import lax
from jax.experimental import pallas as pl
from jax.experimental.pallas import tpu as pltpu
from jax.sharding import PartitionSpec as P

KY = 4
REACH = 4

first_weights = (0.8, -0.2, 4.0 / 105.0, -1.0 / 280.0)
second_weights = (-205.0 / 72.0, 1.6, -0.2, 8.0 / 315.0, -1.0 / 560.0)

FIRST = first_weights[0]
SECOND = second_weights[1]
first_ratio = tuple(w / FIRST for w in first_weights)
second_ratio = tuple(w / SECOND for w in second_weights[1:])

VMEM_LIMIT = 60 * 1024 * 1024

smem = pl.BlockSpec(memory_space=pltpu.SMEM)
vmem = pl.BlockSpec(memory_space=pltpu.VMEM)
anywhere = pl.BlockSpec(memory_space=pl.ANY)


def z_matrix(size):
    second = np.zeros((size, size))
    first = np.zeros((size, size))
    for r in range(1, REACH + 1):
        for z in range(size):
            if z + r < size:
                second[z + r, z] = second_ratio[r - 1]
                first[z + r, z] = first_ratio[r - 1]
            if z - r >= 0:
                second[z - r, z] = second_ratio[r - 1]
                first[z - r, z] = -first_ratio[r - 1]
    whole = np.concatenate([second, first], axis=1).astype(np.float32)
    high = whole.astype(jnp.bfloat16)
    low = (whole - high.astype(np.float32)).astype(jnp.bfloat16)
    return np.concatenate([high, high, low, low], axis=0)


def xor_swap(block, axis, bits):
    size = lax.axis_size(axis)
    return lax.ppermute(block, axis, [(i, i ^ bits) for i in range(size)])


def slabs_of(block):
    size = lax.axis_size("dom")
    if size == 1:
        return [block]
    if size == 2:
        return [block, xor_swap(block, "dom", 1)]
    hops = 2
    up = [(i, i + 1) for i in range(size - 1)]
    down = [(i + 1, i) for i in range(size - 1)]
    found = [block]
    left = right = block
    for _ in range(hops):
        left = lax.ppermute(left, "dom", up)
        right = lax.ppermute(right, "dom", down)
        found = [left] + found + [right]
    return found


def pack_kernel(owners, columns, slots, meta, prints, owner_map, velocity, density, *outs):
    stored = velocity.shape[0]
    me = meta[0]
    first = meta[2] == 0
    for b in range(owners):

        def place(m, count, b=b):
            row = owner_map[prints[b, m]]
            mine = row // (stored * columns) == me
            local = row % stored

            @pl.when(mine)
            def _():
                outs[b][count] = jnp.where(first, velocity[local], density[local])

            return count + mine.astype(jnp.int32)

        lax.fori_loop(0, slots, place, jnp.int32(0))


def unpack_kernel(owners, columns, slots, stored, meta, prints, owner_map, *refs):
    blocks, out = refs[:-1], refs[-1]
    me = meta[0]
    brick_x, brick_y = blocks[0].shape[1:3]
    for b in range(owners):

        def place(m, count, b=b):
            row = owner_map[prints[0, m]]
            mine = row // (stored * columns) == me ^ b

            @pl.when(mine)
            def _():
                x = pl.multiple_of(m // KY * brick_x, brick_x)
                y = pl.multiple_of(m % KY * brick_y, brick_y)
                out[pl.ds(x, brick_x), pl.ds(y, brick_y), :] = blocks[b][count]

            return count + mine.astype(jnp.int32)

        lax.fori_loop(0, slots, place, jnp.int32(0))


def along_x(load, t, i):
    sums, slopes = [], []
    for r in range(1, REACH + 1):
        ahead, behind = load(i + r, t), load(i - r, t)
        sums.append(ahead + behind)
        slopes.append(ahead - behind)
    return sums, slopes


def along_y(rows, ups, downs, t):
    sums, slopes = [], []
    for r in range(1, REACH + 1):
        ahead = rows[t + r] if t + r < 4 else ups[t + r - 4]
        behind = rows[t - r] if t - r >= 0 else downs[t - r + 4]
        sums.append(ahead + behind)
        slopes.append(ahead - behind)
    return sums, slopes


def weigh(parts, ratios):
    total = parts[0]
    for part, ratio in zip(parts[1:], ratios[1:]):
        total = total + ratio * part
    return total


def shifted_rows(rows, sublane):
    ups = [jnp.where(sublane == 7, 0.0, pltpu.roll(row, 7, 0)) for row in rows]
    downs = [jnp.where(sublane == 0, 0.0, pltpu.roll(row, 1, 0)) for row in rows]
    return ups, downs


def split_rows(value):
    high = value.astype(jnp.bfloat16)
    low = (value - high.astype(jnp.float32)).astype(jnp.bfloat16)
    both = jnp.concatenate([high, low], axis=1)
    return jnp.concatenate([both, both], axis=1)


def steps_kernel(count_slabs, own_lo, flipped, inject_lo, meta, zmat, inject_a, inject_b, *refs):
    states = refs[:count_slabs]
    mine = refs[count_slabs : 2 * count_slabs]
    theirs = refs[2 * count_slabs : 3 * count_slabs]
    rims = refs[3 * count_slabs : 4 * count_slabs]
    keep, send = refs[4 * count_slabs : 4 * count_slabs + 2]
    field, logs, square, centre, gx, gy, gz, pulses, sems = refs[4 * count_slabs + 2 :]
    thick = states[0].shape[1]
    steps = rims[0].shape[0]
    lanes = states[0].shape[3]
    window = thick * count_slabs
    own_hi = own_lo + thick
    column = meta[1]
    is_source = meta[2] == 0
    limit = meta[3]
    sublane = lax.broadcasted_iota(jnp.int32, (8, lanes), 0)
    half_of = meta[2]
    reversed_x = flipped & (column == 1)

    def global_x(w):
        if flipped:
            return jnp.where(column == 1, window - 1 - w, w)
        return w + column * thick - own_lo

    def active(w):
        x = global_x(w)
        return (x >= 0) & (x < limit)

    def local_x(v):
        return jnp.where(reversed_x, thick - 1 - v, v)

    def z_parts(load, width):
        rows = jnp.concatenate([load(i, t) for i in range(width) for t in range(4)], axis=0)
        return jnp.dot(split_rows(rows), zmat[...], preferred_element_type=jnp.float32)

    def lo_of(k):
        return jnp.maximum(0, own_lo - REACH * (steps - 1 - k))

    def hi_of(k):
        return jnp.minimum(window, own_hi + REACH * (steps - 1 - k))

    early = inject_a.shape[0]
    rows_b = inject_b.shape[1]

    def copy_a(k, slot):
        return pltpu.make_async_copy(inject_a.at[k], pulses.at[slot], sems.at[slot])

    def copy_b(k, slot):
        return pltpu.make_async_copy(
            inject_b.at[k - early],
            pulses.at[slot, pl.ds(inject_lo, rows_b)],
            sems.at[slot],
        )

    def start_copy(k, slot):
        @pl.when(k < early)
        def _():
            copy_a(k, slot).start()

        @pl.when((k >= early) & (k < steps))
        def _():
            copy_b(k, slot).start()

    def wait_copy(k, slot):
        @pl.when(k < early)
        def _():
            copy_a(k, slot).wait()

        @pl.when(k >= early)
        def _():
            copy_b(k, slot).wait()

    copy_a(0, 0).start()

    zero = jnp.zeros((REACH, 4, 8, lanes), jnp.float32)
    for level in range(2):
        field[level, 0:REACH] = zero
        field[level, REACH + window : 2 * REACH + window] = zero
    logs[0:REACH] = zero
    logs[REACH + window : 2 * REACH + window] = zero

    for s in range(count_slabs):

        def fill(v, carry, s=s):
            w = s * thick + v
            x = local_x(v)
            on = active(w)
            for t in range(4):
                rows = pl.ds(t, 8, stride=4)
                field[0, REACH + w, t] = states[s][0, x, rows, :]
                field[1, REACH + w, t] = states[s][1, x, rows, :]
                a = mine[s][x, rows, :]
                b = theirs[s][x, rows, :]
                courant = jnp.where(is_source, a, b)
                density = jnp.where(is_source, b, a)
                squared = jnp.where(on, courant * courant, 0.0)
                square[w, t] = SECOND * squared
                centre[w, t] = 2.0 + (3.0 * second_weights[0]) * squared
                logs[REACH + w, t] = jnp.where(on, jnp.log(jnp.where(on, density, 1.0)), 0.0)
            return carry

        lax.fori_loop(0, thick, fill, 0)

    def bend(b, carry):
        w = b * 4

        def load(i, t):
            return logs[REACH + w + i, t]

        zs = z_parts(load, 4)
        for i in range(4):
            rows = [load(i, t) for t in range(4)]
            ups, downs = shifted_rows(rows, sublane)
            for t in range(4):
                scale = (FIRST * FIRST / SECOND) * square[w + i, t]
                at = (i * 4 + t) * 8
                gx[w + i, t] = scale * weigh(along_x(load, t, i)[1], first_ratio)
                gy[w + i, t] = scale * weigh(along_y(rows, ups, downs, t)[1], first_ratio)
                gz[w + i, t] = scale * zs[at : at + 8, lanes : 2 * lanes]
        return carry

    lax.fori_loop(0, window // 4, bend, 0)

    rim_low = (sublane == 0) & is_source
    rim_high = (sublane == 7) & is_source

    def one_step(k, carry):
        old = lax.rem(k, 2)
        new = 1 - old
        slot = lax.rem(k, 2)
        wait_copy(k, slot)
        start_copy(k + 1, 1 - slot)

        def block(b, carry):
            w = b * 4
            on = active(w)

            @pl.when(on)
            def _():
                def load(i, t):
                    return field[new, REACH + w + i, t]

                zs = z_parts(load, 4)
                for i in range(4):
                    rows = [load(i, t) for t in range(4)]
                    ups, downs = shifted_rows(rows, sublane)
                    for t in range(4):
                        sx, dx = along_x(load, t, i)
                        sy, dy = along_y(rows, ups, downs, t)
                        at = (i * 4 + t) * 8
                        laplace = weigh([p + q for p, q in zip(sx, sy)], second_ratio)
                        laplace = laplace + zs[at : at + 8, 0:lanes]
                        value = centre[w + i, t] * rows[t] - field[old, REACH + w + i, t]
                        value = value + square[w + i, t] * laplace
                        value = value - gx[w + i, t] * weigh(dx, first_ratio)
                        value = value - gy[w + i, t] * weigh(dy, first_ratio)
                        value = value - gz[w + i, t] * zs[at : at + 8, lanes : 2 * lanes]
                        row = pl.multiple_of(w * 32 + at, 8)
                        value = value + pulses[slot, pl.ds(row, 8), :]
                        field[old, REACH + w + i, t] = value

            @pl.when(jnp.logical_not(on))
            def _():
                field[old, pl.ds(REACH + w, 4)] = jnp.zeros((4, 4, 8, lanes), jnp.float32)

            return carry

        lax.fori_loop(lo_of(k) // 4, hi_of(k) // 4, block, 0)

        @pl.when(is_source)
        def _():
            for s in range(count_slabs):
                first = jnp.maximum(lo_of(k) - s * thick, 0)
                last = jnp.minimum(hi_of(k) - s * thick, thick)

                def rim(v, carry, s=s):
                    w = s * thick + v
                    x = local_x(v)
                    on = active(w)
                    low = jnp.broadcast_to(rims[s][k, 0, pl.ds(x, 1), :], (8, lanes))
                    high = jnp.broadcast_to(rims[s][k, 1, pl.ds(x, 1), :], (8, lanes))
                    field[old, REACH + w, 0] = jnp.where(
                        rim_low & on, low, field[old, REACH + w, 0]
                    )
                    field[old, REACH + w, 3] = jnp.where(
                        rim_high & on, high, field[old, REACH + w, 3]
                    )
                    return carry

                lax.fori_loop(first, last, rim, 0)

        def record(b, carry):
            w = REACH + own_lo + b * 4
            block_half = lax.rem(jnp.where(reversed_x, b + 1, b), 2)
            values = field[old, pl.ds(w, 4)]

            @pl.when(block_half == half_of)
            def _():
                keep[k, b // 2] = values

            @pl.when(block_half != half_of)
            def _():
                send[k, b // 2] = values

            return carry

        lax.fori_loop(0, thick // 4, record, 0)
        return carry

    lax.fori_loop(0, steps, one_step, 0)


def image_kernel(owners, columns, slots, stored, flipped, meta, prints, owner_map, keep, got, *refs):
    outs, total, grid = refs[:owners], refs[owners], refs[owners + 1]
    steps, cols = keep.shape[:2]
    me = meta[0]
    reversed_x = flipped & (meta[1] == 1)
    brick_y = outs[0].shape[2]

    def clear(c, carry):
        def add(k, value):
            return value + keep[k, c] * got[k, c]

        total[c] = lax.fori_loop(0, steps, add, jnp.zeros(keep.shape[2:], jnp.float32))
        return carry

    lax.fori_loop(0, cols, clear, 0)
    for c in range(cols):
        to = jnp.where(reversed_x, cols - 1 - c, c)
        for i in range(4):
            layer = to * 4 + jnp.where(reversed_x, 3 - i, i)
            for t in range(4):
                grid[layer, pl.ds(t, 8, stride=4), :] = total[c, i, t]
    for b in range(owners):

        def place(m, count, b=b):
            row = owner_map[prints[0, m]]
            mine = row // (stored * columns) == me ^ b

            @pl.when(mine)
            def _():
                x = pl.multiple_of(m // KY * 4, 4)
                y = pl.multiple_of(m % KY * brick_y, brick_y)
                outs[b][count] = grid[pl.ds(x, 4), pl.ds(y, brick_y), :]

            return count + mine.astype(jnp.int32)

        lax.fori_loop(0, slots, place, jnp.int32(0))


def sum_kernel(owners, columns, slots, stored, meta, prints, owner_map, *refs):
    blocks, out = refs[:-1], refs[-1]
    me = meta[0]
    out[...] = jnp.zeros_like(out)
    for b in range(owners):

        def place(m, count, b=b):
            row = owner_map[prints[b, m]]
            mine = row // (stored * columns) == me
            local = row % stored

            @pl.when(mine)
            def _():
                out[local] += blocks[b][count]

            return count + mine.astype(jnp.int32)

        lax.fori_loop(0, slots, place, jnp.int32(0))


def call(kernel, out_shape, in_specs, out_specs, scratch=(), cost=None):
    return pl.pallas_call(
        kernel,
        out_shape=out_shape,
        in_specs=in_specs,
        out_specs=out_specs,
        scratch_shapes=list(scratch),
        compiler_params=pltpu.CompilerParams(vmem_limit_bytes=VMEM_LIMIT),
        cost_estimate=cost,
    )


def injection(window, column, own_lo, flipped, thick, height, lanes, is_source,
              source_cell, receivers, pulses, recorded):
    steps, spots = recorded.shape
    cells = jnp.where(is_source, jnp.concatenate([source_cell, jnp.full((spots - 1,), -1, jnp.int32)]), receivers)
    source_values = jnp.concatenate([-pulses[:, None], jnp.zeros((steps, spots - 1), jnp.float32)], axis=1)
    values = jnp.where(is_source, source_values, recorded)
    x = cells // (height * lanes)
    y = cells // lanes % height
    z = cells % lanes
    if flipped:
        w = jnp.where(column == 1, window - 1 - x, x)
    else:
        w = x - column * thick + own_lo
    rows = w * height + y % 4 * 8 + y // 4
    rows = jnp.where((cells >= 0) & (w >= 0) & (w < window), rows, -1)
    which_row = (lax.broadcasted_iota(jnp.int32, (window * height, spots), 0) == rows[None, :]).astype(jnp.bfloat16)
    early = steps // 2
    deep = REACH * (steps - 1 - early)
    lo = max(0, own_lo - deep)
    hi = min(window, own_lo + thick + deep)
    which_lane = (z[:, None] == lax.broadcasted_iota(jnp.int32, (spots, lanes), 1)).astype(jnp.float32)
    high = lax.reduce_precision(values, 8, 7)
    low = lax.reduce_precision(values - high, 8, 7)
    both = jnp.concatenate([high, low], axis=1)
    spread = both[:, :, None] * jnp.concatenate([which_lane, which_lane], axis=0)[None]
    spread = spread.astype(jnp.bfloat16)
    twice = jnp.concatenate([which_row, which_row], axis=1)

    def product(rows, spread):
        return jnp.einsum("rp,kpz->krz", rows, spread, preferred_element_type=jnp.float32)

    return (
        product(twice, spread[:early]),
        product(twice[lo * height : hi * height], spread[early:]),
        lo * height,
    )


def per_device(
    velocity,
    density,
    owner_map,
    footprint,
    aperture,
    source_cell,
    receiver_cells,
    wavelet,
    traces,
    states,
    stored_rims,
):
    f32 = jnp.float32
    owners = lax.axis_size("shot")
    columns = lax.axis_size("dom")
    column = lax.axis_index("dom")
    pair = lax.axis_index("pair")
    shot = lax.axis_index("shot")
    stored, brick_x, brick_y, brick_z = velocity.shape
    half_x = brick_x // 2
    slots = footprint.shape[1]
    per_owner = slots // owners
    across = KY
    bricks_x = slots // across
    thick = bricks_x * brick_x
    height = across * brick_y
    lanes = brick_z
    steps = wavelet.shape[1]
    flipped = columns == 2
    meta = jnp.stack(
        [shot.astype(jnp.int32), column.astype(jnp.int32), pair.astype(jnp.int32), aperture[0] * brick_x]
    )

    prints = jnp.concatenate(
        [footprint] + [xor_swap(footprint, "shot", b) for b in range(1, owners)], axis=0
    )
    brick = jax.ShapeDtypeStruct((per_owner, brick_x, brick_y, brick_z), f32)
    packed = call(
        functools.partial(pack_kernel, owners, columns, slots),
        [brick] * owners,
        [smem, smem, smem, vmem, vmem],
        [vmem] * owners,
    )(meta, prints, owner_map, velocity, density)
    bricks = [packed[0]] + [xor_swap(packed[b], "shot", b) for b in range(1, owners)]
    table = call(
        functools.partial(unpack_kernel, owners, columns, slots, stored),
        jax.ShapeDtypeStruct((thick, height, lanes), f32),
        [smem, smem, smem] + [vmem] * owners,
        vmem,
    )(meta, prints, owner_map, *bricks)

    state_slabs = slabs_of(states[0, 0])
    rim_slabs = slabs_of(stored_rims[0])
    mine = slabs_of(table)
    theirs = [xor_swap(slab, "pair", 1) for slab in mine]

    count = len(mine)
    own_lo = 0 if flipped else (count // 2) * thick
    window = count * thick
    inject_a, inject_b, inject_lo = injection(
        window, column, own_lo, flipped, thick, height, lanes, pair == 0,
        source_cell, receiver_cells[0], wavelet[0], traces[0],
    )

    kept = jax.ShapeDtypeStruct((steps, bricks_x, half_x, 4, height // 4, lanes), f32)
    grid = (window, 4, height // 4, lanes)
    padded = (window + 2 * REACH, 4, height // 4, lanes)
    keep, send = call(
        functools.partial(steps_kernel, count, own_lo, flipped, inject_lo),
        [kept, kept],
        [smem, vmem, anywhere, anywhere] + [vmem] * (4 * count),
        [vmem, vmem],
        [
            pltpu.VMEM((2,) + padded, f32),
            pltpu.VMEM(padded, f32),
            pltpu.VMEM(grid, f32),
            pltpu.VMEM(grid, f32),
            pltpu.VMEM(grid, f32),
            pltpu.VMEM(grid, f32),
            pltpu.VMEM(grid, f32),
            pltpu.VMEM((2, window * height, lanes), f32),
            pltpu.SemaphoreType.DMA((2,)),
        ],
    )(meta, z_matrix(lanes), inject_a, inject_b, *state_slabs, *mine, *theirs, *rim_slabs)
    got = xor_swap(send, "pair", 1)

    part = jax.ShapeDtypeStruct((per_owner, half_x, brick_y, brick_z), f32)
    images = call(
        functools.partial(image_kernel, owners, columns, slots, stored, flipped),
        [part] * owners,
        [smem, smem, smem, vmem, vmem],
        [vmem] * owners,
        [
            pltpu.VMEM(kept.shape[1:], f32),
            pltpu.VMEM((bricks_x * half_x, height, lanes), f32),
        ],
    )(meta, prints, owner_map, keep, got)
    returned = [images[0]] + [xor_swap(images[b], "shot", b) for b in range(1, owners)]
    return call(
        functools.partial(sum_kernel, owners, columns, slots, stored),
        jax.ShapeDtypeStruct((stored, half_x, brick_y, brick_z), f32),
        [smem, smem, smem] + [vmem] * owners,
        vmem,
    )(meta, prints, owner_map, *returned)


def solution(mesh):
    placed = (
        P(("groups", "shot", "dom"), None, None, None),
        P(("groups", "shot", "dom"), None, None, None),
        P("groups"),
        P(("groups", "shot"), "dom"),
        P(("groups", "shot")),
        P(("groups", "shot")),
        P(("groups", "shot"), None),
        P(("groups", "shot"), None),
        P(("groups", "shot"), None, None),
        P(("groups", "shot"), "pair", None, "dom", None, None),
        P(("groups", "shot"), None, None, "dom", None),
    )
    return jax.shard_map(
        per_device,
        mesh=mesh,
        in_specs=placed,
        out_specs=P(("groups", "shot", "dom"), "pair", None, None),
        check_vma=False,
    )
```

```python
import functools

import jax
import jax.numpy as jnp
import numpy as np
from jax import lax
from jax.experimental import pallas as pl
from jax.experimental.pallas import tpu as pltpu
from jax.sharding import PartitionSpec as P

KY = 4
REACH = 4

first_weights = (0.8, -0.2, 4.0 / 105.0, -1.0 / 280.0)
second_weights = (-205.0 / 72.0, 1.6, -0.2, 8.0 / 315.0, -1.0 / 560.0)

FIRST = first_weights[0]
SECOND = second_weights[1]
first_ratio = tuple(w / FIRST for w in first_weights)
second_ratio = tuple(w / SECOND for w in second_weights[1:])

SECOND_UNIT = 8064.0
FIRST_UNIT = 672.0
second_whole = (8064.0, -1008.0, 128.0, -9.0)
first_whole = (672.0, -168.0, 32.0, -3.0)

VMEM_LIMIT = 60 * 1024 * 1024

smem = pl.BlockSpec(memory_space=pltpu.SMEM)
vmem = pl.BlockSpec(memory_space=pltpu.VMEM)
anywhere = pl.BlockSpec(memory_space=pl.ANY)


def z_matrix(size):
    second = np.zeros((size, size))
    first = np.zeros((size, size))
    for r in range(1, REACH + 1):
        for z in range(size):
            if z + r < size:
                second[z + r, z] = second_whole[r - 1]
                first[z + r, z] = first_whole[r - 1]
            if z - r >= 0:
                second[z - r, z] = second_whole[r - 1]
                first[z - r, z] = -first_whole[r - 1]
    whole = np.concatenate([second, first], axis=1)
    return np.concatenate([whole, whole], axis=0).astype(jnp.bfloat16)


def xor_swap(block, axis, bits):
    size = lax.axis_size(axis)
    return lax.ppermute(block, axis, [(i, i ^ bits) for i in range(size)])


def slabs_of(block):
    size = lax.axis_size("dom")
    if size == 1:
        return [block]
    if size == 2:
        return [block, xor_swap(block, "dom", 1)]
    hops = 2
    up = [(i, i + 1) for i in range(size - 1)]
    down = [(i + 1, i) for i in range(size - 1)]
    found = [block]
    left = right = block
    for _ in range(hops):
        left = lax.ppermute(left, "dom", up)
        right = lax.ppermute(right, "dom", down)
        found = [left] + found + [right]
    return found


def pack_kernel(owners, columns, slots, meta, prints, owner_map, velocity, density, *outs):
    stored = velocity.shape[0]
    me = meta[0]
    first = meta[2] == 0
    for b in range(owners):

        def place(m, count, b=b):
            row = owner_map[prints[b, m]]
            mine = row // (stored * columns) == me
            local = row % stored

            @pl.when(mine)
            def _():
                outs[b][count] = jnp.where(first, velocity[local], density[local])

            return count + mine.astype(jnp.int32)

        lax.fori_loop(0, slots, place, jnp.int32(0))


def unpack_kernel(owners, columns, slots, stored, meta, prints, owner_map, *refs):
    blocks, out = refs[:-1], refs[-1]
    me = meta[0]
    brick_x, brick_y = blocks[0].shape[1:3]
    for b in range(owners):

        def place(m, count, b=b):
            row = owner_map[prints[0, m]]
            mine = row // (stored * columns) == me ^ b

            @pl.when(mine)
            def _():
                x = pl.multiple_of(m // KY * brick_x, brick_x)
                y = pl.multiple_of(m % KY * brick_y, brick_y)
                out[pl.ds(x, brick_x), pl.ds(y, brick_y), :] = blocks[b][count]

            return count + mine.astype(jnp.int32)

        lax.fori_loop(0, slots, place, jnp.int32(0))


def each(f, *lists):
    return [f(*items) for items in zip(*lists)]


def add(a, b):
    return each(lambda p, q: p + q, a, b)


def sub(a, b):
    return each(lambda p, q: p - q, a, b)


def mul(a, b):
    return each(lambda p, q: p * q, a, b)


def scaled(factor, a):
    return [factor * p for p in a]


def shifted_rows(rows, sublane):
    ups = [jnp.where(sublane == 7, 0.0, pltpu.roll(row, 7, 0)) for row in rows]
    downs = [jnp.where(sublane == 0, 0.0, pltpu.roll(row, 1, 0)) for row in rows]
    return downs + rows + ups


def split_rows(value):
    high = value.astype(jnp.bfloat16)
    low = (value - high.astype(jnp.float32)).astype(jnp.bfloat16)
    return jnp.concatenate([high, low], axis=1)


def steps_kernel(count_slabs, own_lo, flipped, inject_lo, meta, zmat, inject_a, inject_b, *refs):
    states = refs[:count_slabs]
    mine = refs[count_slabs : 2 * count_slabs]
    theirs = refs[2 * count_slabs : 3 * count_slabs]
    rims = refs[3 * count_slabs]
    keep, send = refs[3 * count_slabs + 1 : 3 * count_slabs + 3]
    field, logs, square, centre, gx, gy, gz, pulses, zbuf, record, sems, out_sems = refs[
        3 * count_slabs + 3 :
    ]
    thick = states[0].shape[1]
    steps = rims.shape[0]
    lanes = states[0].shape[3]
    window = thick * count_slabs
    own_hi = own_lo + thick
    cols = thick // 8
    column = meta[1]
    is_source = meta[2] == 0
    limit = meta[3]
    half_of = meta[2]
    sublane = lax.broadcasted_iota(jnp.int32, (8, lanes), 0)
    reversed_x = flipped & (column == 1)
    turn = reversed_x.astype(jnp.int32)

    def global_x(w):
        if flipped:
            return jnp.where(column == 1, window - 1 - w, w)
        return w + column * thick - own_lo

    def rim_x(w):
        if flipped:
            return jnp.where(column == 1, window - 1 - w, w)
        return w

    def active(w):
        x = global_x(w)
        return (x >= 0) & (x < limit)

    def local_x(v):
        return jnp.where(reversed_x, thick - 1 - v, v)

    def z_parts(load):
        rows = jnp.concatenate([load(i, t) for i in range(4) for t in range(4)], axis=0)
        return jnp.dot(split_rows(rows), zmat[...], preferred_element_type=jnp.float32)

    def lo_of(k):
        return jnp.maximum(0, own_lo - REACH * (steps - 1 - k))

    def hi_of(k):
        return jnp.minimum(window, own_hi + REACH * (steps - 1 - k))

    early = inject_a.shape[0]
    rows_b = inject_b.shape[1]

    def copy_a(k, slot):
        return pltpu.make_async_copy(inject_a.at[k], pulses.at[slot], sems.at[slot])

    def copy_b(k, slot):
        return pltpu.make_async_copy(
            inject_b.at[k - early],
            pulses.at[slot, pl.ds(inject_lo, rows_b)],
            sems.at[slot],
        )

    def start_copy(k, slot):
        @pl.when(k < early)
        def _():
            copy_a(k, slot).start()

        @pl.when((k >= early) & (k < steps))
        def _():
            copy_b(k, slot).start()

    def wait_copy(k, slot):
        @pl.when(k < early)
        def _():
            copy_a(k, slot).wait()

        @pl.when(k >= early)
        def _():
            copy_b(k, slot).wait()

    def out_copies(k, slot):
        return [
            pltpu.make_async_copy(
                record.at[slot, pl.ds(0, cols)], keep.at[k], out_sems.at[slot, 0]
            ),
            pltpu.make_async_copy(
                record.at[slot, pl.ds(cols, cols)], send.at[k], out_sems.at[slot, 1]
            ),
        ]

    copy_a(0, 0).start()

    zero = jnp.zeros((REACH, 4, 8, lanes), jnp.float32)
    for level in range(2):
        field[level, 0:REACH] = zero
        field[level, REACH + window : 2 * REACH + window] = zero
    logs[0:REACH] = zero
    logs[REACH + window : 2 * REACH + window] = zero

    for s in range(count_slabs):

        def fill(v, carry, s=s):
            w = s * thick + v
            x = local_x(v)
            on = active(w)
            for t in range(4):
                rows = pl.ds(t, 8, stride=4)
                field[0, REACH + w, t] = states[s][0, x, rows, :]
                field[1, REACH + w, t] = states[s][1, x, rows, :]
                a = mine[s][x, rows, :]
                b = theirs[s][x, rows, :]
                courant = jnp.where(is_source, a, b)
                density = jnp.where(is_source, b, a)
                squared = jnp.where(on, courant * courant, 0.0)
                square[w, t] = SECOND * squared
                centre[w, t] = 2.0 + (3.0 * second_weights[0]) * squared
                logs[REACH + w, t] = jnp.where(on, jnp.log(jnp.where(on, density, 1.0)), 0.0)
            return carry

        lax.fori_loop(0, thick, fill, 0)

    def slopes(load, i, rows):
        dx = dy = None
        for r in range(1, REACH + 1):
            px = sub([load(i + r, t) for t in range(4)], [load(i - r, t) for t in range(4)])
            py = sub(rows[4 + r : 8 + r], rows[4 - r : 8 - r])
            if r == 1:
                dx, dy = px, py
            else:
                dx = add(dx, scaled(first_ratio[r - 1], px))
                dy = add(dy, scaled(first_ratio[r - 1], py))
        return dx, dy

    def bend(b, carry):
        w = b * 4

        def load(i, t):
            return logs[REACH + w + i, t]

        zs = z_parts(load)
        for i in range(4):
            rows = shifted_rows([load(i, t) for t in range(4)], sublane)
            dx, dy = slopes(load, i, rows)
            for t in range(4):
                scale = (FIRST * FIRST / SECOND) * square[w + i, t]
                at = (i * 4 + t) * 8
                gx[w + i, t] = scale * dx[t]
                gy[w + i, t] = scale * dy[t]
                gz[w + i, t] = (scale * (1.0 / (FIRST_UNIT * FIRST_UNIT))) * zs[at : at + 8, lanes:]
        return carry

    lax.fori_loop(0, window // 4, bend, 0)

    rim_low = (sublane == 0) & is_source
    rim_high = (sublane == 7) & is_source

    def one_step(k, carry):
        old = lax.rem(k, 2)
        new = 1 - old
        slot = lax.rem(k, 2)
        wait_copy(k, slot)
        start_copy(k + 1, 1 - slot)

        @pl.when(k >= 2)
        def _():
            for copy in out_copies(k - 2, slot):
                copy.wait()

        first = lo_of(k) // 4
        last = hi_of(k) // 4
        zbuf[lax.rem(first, 2)] = z_parts(lambda i, t: field[new, REACH + first * 4 + i, t])

        def block(b, carry):
            w = b * 4
            on = active(w)
            after = jnp.minimum(b + 1, window // 4 - 1) * 4
            own = b - own_lo // 4
            half = lax.rem(own + turn, 2)
            is_own = (own >= 0) & (own < thick // 4)
            to = jnp.where(is_own, jnp.where(half == half_of, 0, cols) + own // 2, 2 * cols)
            zslot = lax.rem(b, 2)

            @pl.when(on)
            def _():
                def load(i, t):
                    return field[new, REACH + w + i, t]

                zs = z_parts(lambda i, t: field[new, REACH + after + i, t])
                for i in range(4):
                    mid = [load(i, t) for t in range(4)]
                    rows = shifted_rows(mid, sublane)
                    lap = dx = dy = None
                    for r in range(1, REACH + 1):
                        ax = [load(i + r, t) for t in range(4)]
                        bx = [load(i - r, t) for t in range(4)]
                        ay = rows[4 + r : 8 + r]
                        by = rows[4 - r : 8 - r]
                        px = sub(ax, bx)
                        py = sub(ay, by)
                        total = add(add(ax, bx), add(ay, by))
                        if r == 1:
                            lap, dx, dy = total, px, py
                        else:
                            lap = add(lap, scaled(second_ratio[r - 1], total))
                            dx = add(dx, scaled(first_ratio[r - 1], px))
                            dy = add(dy, scaled(first_ratio[r - 1], py))
                    at = [(i * 4 + t) * 8 for t in range(4)]
                    z2 = [zbuf[zslot, a : a + 8, 0:lanes] for a in at]
                    z1 = [zbuf[zslot, a : a + 8, lanes:] for a in at]
                    lap = add(lap, scaled(1.0 / SECOND_UNIT, z2))
                    value = sub(
                        mul([centre[w + i, t] for t in range(4)], mid),
                        [field[old, REACH + w + i, t] for t in range(4)],
                    )
                    row = pl.multiple_of(w * 32 + i * 32, 32)
                    value = add(value, [pulses[slot, pl.ds(row + t * 8, 8), :] for t in range(4)])
                    value = add(value, mul([square[w + i, t] for t in range(4)], lap))
                    drift = mul([gx[w + i, t] for t in range(4)], dx)
                    drift = add(drift, mul([gy[w + i, t] for t in range(4)], dy))
                    drift = add(drift, mul([gz[w + i, t] for t in range(4)], z1))
                    value = sub(value, drift)
                    x = rim_x(w + i)
                    low = jnp.broadcast_to(rims[k, 0, pl.ds(x, 1), :], (8, lanes))
                    high = jnp.broadcast_to(rims[k, 1, pl.ds(x, 1), :], (8, lanes))
                    value[0] = jnp.where(rim_low, low, value[0])
                    value[3] = jnp.where(rim_high, high, value[3])
                    for t in range(4):
                        field[old, REACH + w + i, t] = value[t]
                        record[slot, to, i, t] = value[t]
                zbuf[1 - zslot] = zs

            @pl.when(jnp.logical_not(on))
            def _():
                nothing = jnp.zeros((4, 4, 8, lanes), jnp.float32)
                field[old, pl.ds(REACH + w, 4)] = nothing
                record[slot, to] = nothing
                zbuf[1 - zslot] = z_parts(lambda i, t: field[new, REACH + after + i, t])

            return carry

        lax.fori_loop(first, last, block, 0)
        for copy in out_copies(k, slot):
            copy.start()
        return carry

    lax.fori_loop(0, steps, one_step, 0)
    for k in (steps - 2, steps - 1):
        for copy in out_copies(k, k % 2):
            copy.wait()


def image_kernel(owners, columns, slots, stored, flipped, meta, prints, owner_map, keep, got, *refs):
    outs, total, grid = refs[:owners], refs[owners], refs[owners + 1]
    steps, cols = keep.shape[:2]
    me = meta[0]
    reversed_x = flipped & (meta[1] == 1)
    brick_y = outs[0].shape[2]

    def clear(c, carry):
        def add(k, value):
            return value + keep[k, c] * got[k, c]

        total[c] = lax.fori_loop(0, steps, add, jnp.zeros(keep.shape[2:], jnp.float32))
        return carry

    lax.fori_loop(0, cols, clear, 0)
    for c in range(cols):
        to = jnp.where(reversed_x, cols - 1 - c, c)
        for i in range(4):
            layer = to * 4 + jnp.where(reversed_x, 3 - i, i)
            for t in range(4):
                grid[layer, pl.ds(t, 8, stride=4), :] = total[c, i, t]
    for b in range(owners):

        def place(m, count, b=b):
            row = owner_map[prints[0, m]]
            mine = row // (stored * columns) == me ^ b

            @pl.when(mine)
            def _():
                x = pl.multiple_of(m // KY * 4, 4)
                y = pl.multiple_of(m % KY * brick_y, brick_y)
                outs[b][count] = grid[pl.ds(x, 4), pl.ds(y, brick_y), :]

            return count + mine.astype(jnp.int32)

        lax.fori_loop(0, slots, place, jnp.int32(0))


def sum_kernel(owners, columns, slots, stored, meta, prints, owner_map, *refs):
    blocks, out = refs[:-1], refs[-1]
    me = meta[0]
    out[...] = jnp.zeros_like(out)
    for b in range(owners):

        def place(m, count, b=b):
            row = owner_map[prints[b, m]]
            mine = row // (stored * columns) == me
            local = row % stored

            @pl.when(mine)
            def _():
                out[local] += blocks[b][count]

            return count + mine.astype(jnp.int32)

        lax.fori_loop(0, slots, place, jnp.int32(0))


def call(kernel, out_shape, in_specs, out_specs, scratch=(), cost=None):
    return pl.pallas_call(
        kernel,
        out_shape=out_shape,
        in_specs=in_specs,
        out_specs=out_specs,
        scratch_shapes=list(scratch),
        compiler_params=pltpu.CompilerParams(vmem_limit_bytes=VMEM_LIMIT),
        cost_estimate=cost,
    )


def run_steps(
    count, own_lo, flipped, inject_lo, steps, meta, inject_a, inject_b, state_slabs, mine, theirs, rims
):
    f32 = jnp.float32
    thick, height, lanes = mine[0].shape
    cols = thick // 8
    window = count * thick
    kept = jax.ShapeDtypeStruct((steps, cols, 4, 4, height // 4, lanes), f32)
    grid = (window, 4, height // 4, lanes)
    padded = (window + 2 * REACH, 4, height // 4, lanes)
    return call(
        functools.partial(steps_kernel, count, own_lo, flipped, inject_lo),
        [kept, kept],
        [smem, vmem, anywhere, anywhere] + [vmem] * (3 * count + 1),
        [anywhere, anywhere],
        [
            pltpu.VMEM((2,) + padded, f32),
            pltpu.VMEM(padded, f32),
            pltpu.VMEM(grid, f32),
            pltpu.VMEM(grid, f32),
            pltpu.VMEM(grid, f32),
            pltpu.VMEM(grid, f32),
            pltpu.VMEM(grid, f32),
            pltpu.VMEM((2, window * height, lanes), f32),
            pltpu.VMEM((2, 128, 2 * lanes), f32),
            pltpu.VMEM((2, 2 * cols + 1, 4, 4, height // 4, lanes), f32),
            pltpu.SemaphoreType.DMA((2,)),
            pltpu.SemaphoreType.DMA((2, 2)),
        ],
    )(meta, z_matrix(lanes), inject_a, inject_b, *state_slabs, *mine, *theirs, rims)


def injection(window, column, own_lo, flipped, thick, height, lanes, is_source,
              source_cell, receivers, pulses, recorded):
    steps, spots = recorded.shape
    cells = jnp.where(is_source, jnp.concatenate([source_cell, jnp.full((spots - 1,), -1, jnp.int32)]), receivers)
    source_values = jnp.concatenate([-pulses[:, None], jnp.zeros((steps, spots - 1), jnp.float32)], axis=1)
    values = jnp.where(is_source, source_values, recorded)
    x = cells // (height * lanes)
    y = cells // lanes % height
    z = cells % lanes
    if flipped:
        w = jnp.where(column == 1, window - 1 - x, x)
    else:
        w = x - column * thick + own_lo
    rows = w * height + y % 4 * 8 + y // 4
    rows = jnp.where((cells >= 0) & (w >= 0) & (w < window), rows, -1)
    which_row = (lax.broadcasted_iota(jnp.int32, (window * height, spots), 0) == rows[None, :]).astype(jnp.bfloat16)
    early = steps // 2
    deep = REACH * (steps - 1 - early)
    lo = max(0, own_lo - deep)
    hi = min(window, own_lo + thick + deep)
    which_lane = (z[:, None] == lax.broadcasted_iota(jnp.int32, (spots, lanes), 1)).astype(jnp.float32)
    high = lax.reduce_precision(values, 8, 7)
    low = lax.reduce_precision(values - high, 8, 7)
    both = jnp.concatenate([high, low], axis=1)
    spread = both[:, :, None] * jnp.concatenate([which_lane, which_lane], axis=0)[None]
    spread = spread.astype(jnp.bfloat16)
    twice = jnp.concatenate([which_row, which_row], axis=1)

    def product(rows, spread):
        return jnp.einsum("rp,kpz->krz", rows, spread, preferred_element_type=jnp.float32)

    return (
        product(twice, spread[:early]),
        product(twice[lo * height : hi * height], spread[early:]),
        lo * height,
    )


def per_device(
    velocity,
    density,
    owner_map,
    footprint,
    aperture,
    source_cell,
    receiver_cells,
    wavelet,
    traces,
    states,
    stored_rims,
):
    f32 = jnp.float32
    owners = lax.axis_size("shot")
    columns = lax.axis_size("dom")
    column = lax.axis_index("dom")
    pair = lax.axis_index("pair")
    shot = lax.axis_index("shot")
    stored, brick_x, brick_y, brick_z = velocity.shape
    half_x = brick_x // 2
    slots = footprint.shape[1]
    per_owner = slots // owners
    across = KY
    bricks_x = slots // across
    thick = bricks_x * brick_x
    height = across * brick_y
    lanes = brick_z
    steps = wavelet.shape[1]
    flipped = columns == 2
    meta = jnp.stack(
        [shot.astype(jnp.int32), column.astype(jnp.int32), pair.astype(jnp.int32), aperture[0] * brick_x]
    )

    prints = jnp.concatenate(
        [footprint] + [xor_swap(footprint, "shot", b) for b in range(1, owners)], axis=0
    )
    brick = jax.ShapeDtypeStruct((per_owner, brick_x, brick_y, brick_z), f32)
    packed = call(
        functools.partial(pack_kernel, owners, columns, slots),
        [brick] * owners,
        [smem, smem, smem, vmem, vmem],
        [vmem] * owners,
    )(meta, prints, owner_map, velocity, density)
    bricks = [packed[0]] + [xor_swap(packed[b], "shot", b) for b in range(1, owners)]
    table = call(
        functools.partial(unpack_kernel, owners, columns, slots, stored),
        jax.ShapeDtypeStruct((thick, height, lanes), f32),
        [smem, smem, smem] + [vmem] * owners,
        vmem,
    )(meta, prints, owner_map, *bricks)

    state_slabs = slabs_of(states[0, 0])
    rim_slabs = slabs_of(stored_rims[0])
    if flipped:
        rims = jnp.where(
            column == 1,
            jnp.concatenate(rim_slabs[::-1], axis=2),
            jnp.concatenate(rim_slabs, axis=2),
        )
    else:
        rims = jnp.concatenate(rim_slabs, axis=2)
    mine = slabs_of(table)
    theirs = [xor_swap(slab, "pair", 1) for slab in mine]

    count = len(mine)
    own_lo = 0 if flipped else (count // 2) * thick
    window = count * thick
    inject_a, inject_b, inject_lo = injection(
        window, column, own_lo, flipped, thick, height, lanes, pair == 0,
        source_cell, receiver_cells[0], wavelet[0], traces[0],
    )

    keep, send = run_steps(
        count, own_lo, flipped, inject_lo, steps, meta, inject_a, inject_b, state_slabs, mine, theirs, rims
    )
    got = xor_swap(send, "pair", 1)

    part = jax.ShapeDtypeStruct((per_owner, half_x, brick_y, brick_z), f32)
    images = call(
        functools.partial(image_kernel, owners, columns, slots, stored, flipped),
        [part] * owners,
        [smem, smem, smem, vmem, vmem],
        [vmem] * owners,
        [
            pltpu.VMEM(keep.shape[1:], f32),
            pltpu.VMEM((bricks_x * half_x, height, lanes), f32),
        ],
    )(meta, prints, owner_map, keep, got)
    returned = [images[0]] + [xor_swap(images[b], "shot", b) for b in range(1, owners)]
    return call(
        functools.partial(sum_kernel, owners, columns, slots, stored),
        jax.ShapeDtypeStruct((stored, half_x, brick_y, brick_z), f32),
        [smem, smem, smem] + [vmem] * owners,
        vmem,
    )(meta, prints, owner_map, *returned)


def solution(mesh):
    placed = (
        P(("groups", "shot", "dom"), None, None, None),
        P(("groups", "shot", "dom"), None, None, None),
        P("groups"),
        P(("groups", "shot"), "dom"),
        P(("groups", "shot")),
        P(("groups", "shot")),
        P(("groups", "shot"), None),
        P(("groups", "shot"), None),
        P(("groups", "shot"), None, None),
        P(("groups", "shot"), "pair", None, "dom", None, None),
        P(("groups", "shot"), None, None, "dom", None),
    )
    return jax.shard_map(
        per_device,
        mesh=mesh,
        in_specs=placed,
        out_specs=P(("groups", "shot", "dom"), "pair", None, None),
        check_vma=False,
    )
```

```python
import functools

import jax
import jax.numpy as jnp
import numpy as np
from jax import lax
from jax.experimental import pallas as pl
from jax.experimental.pallas import tpu as pltpu
from jax.sharding import PartitionSpec as P

KY = 4
REACH = 4

first_weights = (0.8, -0.2, 4.0 / 105.0, -1.0 / 280.0)
second_weights = (-205.0 / 72.0, 1.6, -0.2, 8.0 / 315.0, -1.0 / 560.0)

FIRST = first_weights[0]
SECOND = second_weights[1]
first_ratio = tuple(w / FIRST for w in first_weights)
second_ratio = tuple(w / SECOND for w in second_weights[1:])

SECOND_UNIT = 8064.0
FIRST_UNIT = 672.0
second_whole = (8064.0, -1008.0, 128.0, -9.0)
first_whole = (672.0, -168.0, 32.0, -3.0)

HOPS = 2
MIB = 1024 * 1024

smem = pl.BlockSpec(memory_space=pltpu.SMEM)
vmem = pl.BlockSpec(memory_space=pltpu.VMEM)
anywhere = pl.BlockSpec(memory_space=pl.ANY)


def z_matrix(size):
    second = np.zeros((size, size))
    first = np.zeros((size, size))
    for r in range(1, REACH + 1):
        for z in range(size):
            if z + r < size:
                second[z + r, z] = second_whole[r - 1]
                first[z + r, z] = first_whole[r - 1]
            if z - r >= 0:
                second[z - r, z] = second_whole[r - 1]
                first[z - r, z] = -first_whole[r - 1]
    whole = np.concatenate([second, first], axis=1)
    return np.concatenate([whole, whole], axis=0).astype(jnp.bfloat16)


def y_matrix(across, layers):
    second = np.zeros((across, across))
    first = np.zeros((across, across))
    for r in range(1, REACH + 1):
        for y in range(across):
            if y + r < across:
                second[y, y + r] = second_whole[r - 1]
                first[y, y + r] = first_whole[r - 1]
            if y - r >= 0:
                second[y, y - r] = second_whole[r - 1]
                first[y, y - r] = -first_whole[r - 1]
    same = np.eye(layers)
    whole = np.concatenate([np.kron(same, second), np.kron(same, first)], axis=0)
    return np.concatenate([whole, whole], axis=1).astype(jnp.bfloat16)


def xor_swap(block, axis, bits):
    size = lax.axis_size(axis)
    return lax.ppermute(block, axis, [(i, i ^ bits) for i in range(size)])


def slabs_of(block, first_only=False):
    size = lax.axis_size("dom")
    pairs = lax.axis_size("pair")

    def shift(x, moves):
        if first_only:
            return lax.ppermute(x, ("dom", "pair"), [(i * pairs, j * pairs) for i, j in moves])
        return lax.ppermute(x, "dom", moves)

    if size == 1:
        return [block]
    if size == 2:
        return [block, shift(block, [(0, 1), (1, 0)])]
    up = [(i, i + 1) for i in range(size - 1)]
    down = [(i + 1, i) for i in range(size - 1)]
    found = [block]
    left = right = block
    for _ in range(HOPS):
        left = shift(left, up)
        right = shift(right, down)
        found = [left] + found + [right]
    return found


def serve(prints, owner_map, base, stored, take):
    slots = prints.shape[1]

    def one(m, count):
        local = owner_map[prints[0, m]] - base
        mine = (local >= 0) & (local < stored)

        @pl.when(mine)
        def _():
            take(m, local, count)

        return count + mine.astype(jnp.int32)

    lax.fori_loop(0, slots, one, jnp.int32(0))


def pack_kernel(owners, columns, relay, meta, owner_map, *refs):
    prints, refs = refs[:owners], refs[owners:]
    if relay:
        (table,), refs = refs[:1], refs[1:]
        column = 1 - meta[1]
    else:
        (velocity, density), refs = refs[:2], refs[2:]
        table = velocity
        column = meta[1]
    outs, sems = refs[:-1], refs[-1]
    stored = table.shape[0]
    per_owner = outs[0].shape[0]
    first = meta[2] == 0
    base = (meta[0] * columns + column) * stored

    def send(source, local, out, rank, sem):
        pltpu.make_async_copy(source.at[local], out.at[rank], sem).start()

    for b in range(owners):

        def take(m, local, rank, b=b):
            if relay:
                send(table, local, outs[b], rank, sems.at[b, rank])
                return

            @pl.when(first)
            def _():
                send(velocity, local, outs[b], rank, sems.at[b, rank])
                if b == 0:
                    send(density, local, outs[owners], rank, sems.at[owners, rank])

            @pl.when(jnp.logical_not(first))
            def _():
                send(density, local, outs[b], rank, sems.at[b, rank])
                if b == 0:
                    send(velocity, local, outs[owners], rank, sems.at[owners, rank])

        serve(prints[b], owner_map, base, stored, take)
    for b, out in enumerate(outs):
        for rank in range(per_owner):
            pltpu.make_async_copy(table.at[0], out.at[rank], sems.at[b, rank]).wait()


def unpack_kernel(owners, columns, stored, meta, owner_map, prints, *refs):
    blocks, out = refs[:-1], refs[-1]
    for b in range(owners):
        base = ((meta[0] ^ b) * columns + meta[1]) * stored

        def take(m, local, rank, b=b):
            out[m] = blocks[b][rank]

        serve(prints, owner_map, base, stored, take)


def each(f, *lists):
    return [f(*items) for items in zip(*lists)]


def add(a, b):
    return each(lambda p, q: p + q, a, b)


def sub(a, b):
    return each(lambda p, q: p - q, a, b)


def mul(a, b):
    return each(lambda p, q: p * q, a, b)


def scaled(factor, a):
    return [factor * p for p in a]


def along_x(column):
    size = len(column) - 2 * REACH
    lap = slope = None
    for r in range(1, REACH + 1):
        ahead = column[REACH + r : REACH + r + size]
        behind = column[REACH - r : REACH - r + size]
        total, apart = add(ahead, behind), sub(ahead, behind)
        if r == 1:
            lap, slope = total, apart
        else:
            lap = add(lap, scaled(second_ratio[r - 1], total))
            slope = add(slope, scaled(first_ratio[r - 1], apart))
    return lap, slope


def y_and_z(value, zmat, ymat, zout, youts):
    high = value.astype(jnp.bfloat16)
    low = (value - high.astype(jnp.float32)).astype(jnp.bfloat16)
    z = jnp.dot(
        jnp.concatenate([high, low], axis=1), zmat[...], preferred_element_type=jnp.float32
    )
    ys = []
    group = ymat.shape[0] // 2
    for at in range(0, value.shape[0], group):
        both = jnp.concatenate([high[at : at + group], low[at : at + group]], axis=0)
        ys.append(jnp.dot(ymat[...], both, preferred_element_type=jnp.float32))
    return z, ys


BLOCK = 8


def steps_kernel(shape, meta, owner_map, zmat, ymat, inject_a, inject_b, *refs):
    owners, columns, stored, sides, inject_lo = shape
    if sides:
        own_prints, other_prints = refs[:2]
        refs = refs[2:]
    count = 2 if sides else 2 * HOPS + 1
    parts = owners if sides else 1
    mine = [refs[c * parts : (c + 1) * parts] for c in range(count)]
    refs = refs[count * parts :]
    theirs = [refs[c * parts : (c + 1) * parts] for c in range(count)]
    refs = refs[count * parts :]
    states, refs = refs[:count], refs[count:]
    rims, refs = refs[:count], refs[count:]
    keep, send = refs[:2]
    field, logs, square, centre, gx, gy, gz, pulses, zbuf, ybuf, record, rim, sems, out_sems, in_sems = refs[2:]
    thick, height, lanes = states[0].shape[1:]
    steps = rims[0].shape[0]
    window = thick * count
    cols = thick // 8
    rows8 = height // 8
    column = meta[1]
    is_source = meta[2] == 0
    limit = meta[3]
    half_of = meta[2]
    sublane = lax.broadcasted_iota(jnp.int32, (8, lanes), 0)
    if sides:
        own_lo = column * thick
        places = [column * thick, (1 - column) * thick]
    else:
        own_lo = HOPS * thick
        places = [s * thick for s in range(count)]

    def active(w):
        x = w if sides else w + column * thick - own_lo
        return (x >= 0) & (x < limit)

    def lo_of(k):
        return jnp.maximum(0, own_lo - REACH * (steps - 1 - k))

    def hi_of(k):
        return jnp.minimum(window, own_lo + thick + REACH * (steps - 1 - k))

    early = inject_a.shape[0]
    rows_b = inject_b.shape[1]

    def copy_a(k, slot):
        return pltpu.make_async_copy(inject_a.at[k], pulses.at[slot], sems.at[slot])

    def copy_b(k, slot):
        return pltpu.make_async_copy(
            inject_b.at[k - early],
            pulses.at[slot, pl.ds(inject_lo, rows_b)],
            sems.at[slot],
        )

    def start_copy(k, slot):
        @pl.when(k < early)
        def _():
            copy_a(k, slot).start()

        @pl.when((k >= early) & (k < steps))
        def _():
            copy_b(k, slot).start()

    def wait_copy(k, slot):
        @pl.when(k < early)
        def _():
            copy_a(k, slot).wait()

        @pl.when(k >= early)
        def _():
            copy_b(k, slot).wait()

    def out_copies(k, slot):
        return [
            pltpu.make_async_copy(
                record.at[slot, pl.ds(0, cols)], keep.at[k], out_sems.at[slot, 0]
            ),
            pltpu.make_async_copy(
                record.at[slot, pl.ds(cols, cols)], send.at[k], out_sems.at[slot, 1]
            ),
        ]

    def in_copies(s):
        place = places[s] if isinstance(places[s], int) else pl.multiple_of(places[s], 8)
        copies = [
            pltpu.make_async_copy(
                states[s].at[level], field.at[level, pl.ds(REACH + place, thick)], in_sems.at[s, level]
            )
            for level in range(2)
        ]
        return copies + [
            pltpu.make_async_copy(rims[s], rim.at[:, :, pl.ds(place, thick), :], in_sems.at[s, 2])
        ]

    copy_a(0, 0).start()
    for s in range(count):
        for copy in in_copies(s):
            copy.start()

    zero = jnp.zeros((REACH, height, lanes), jnp.float32)
    for level in range(2):
        field[level, 0:REACH] = zero
        field[level, REACH + window : 2 * REACH + window] = zero
    logs[0:REACH] = zero
    logs[REACH + window : 2 * REACH + window] = zero

    for s in range(count):

        def fill(m, a, b, rank, direct, s=s):
            x0 = places[s] + (m // KY) * 8
            y0 = pl.multiple_of((m % KY) * 8, 8)
            on = active(x0)
            for i in range(8):
                courant = jnp.where(is_source, a[rank, i], b[rank, i])
                density = jnp.where(is_source, b[rank, i], a[rank, i])
                squared = jnp.where(on, courant * courant, 0.0)
                square[x0 + i, pl.ds(y0, 8), :] = SECOND * squared
                centre[x0 + i, pl.ds(y0, 8), :] = 2.0 + (3.0 * second_weights[0]) * squared
                logs[REACH + x0 + i, pl.ds(y0, 8), :] = jnp.where(
                    on, jnp.log(jnp.where(on, density, 1.0)), 0.0
                )

        if sides:
            prints = (own_prints, other_prints)[s]
            for b in range(owners):
                base = ((meta[0] ^ b) * columns + (column if s == 0 else 1 - column)) * stored

                def take(m, local, rank, b=b, s=s):
                    fill(m, mine[s][b], theirs[s][b], rank, False)

                serve(prints, owner_map, base, stored, take)
        else:

            def one(m, carry, s=s):
                fill(m, mine[s][0], theirs[s][0], m, False)
                return carry

            lax.fori_loop(0, mine[s][0].shape[0], one, 0)

    def bend(b, carry):
        w = b * 4
        z, ys = y_and_z(
            logs[pl.ds(REACH + w, 4)].reshape(4 * height, lanes), zmat, ymat, None, None
        )
        for q in range(rows8):
            part = slice(q * 8, q * 8 + 8)
            _, slope = along_x([logs[w + j, part, :] for j in range(4 + 2 * REACH)])
            for i in range(4):
                at = i * height + q * 8
                scale = (FIRST * FIRST / SECOND) * square[w + i, part, :]
                whole = scale * (1.0 / (FIRST_UNIT * FIRST_UNIT))
                gx[w + i, part, :] = scale * slope[i]
                gy[w + i, part, :] = whole * ys[0][4 * height + at : 4 * height + at + 8]
                gz[w + i, part, :] = whole * z[at : at + 8, lanes:]
        return carry

    lax.fori_loop(0, window // 4, bend, 0)
    for s in range(count):
        for copy in in_copies(s):
            copy.wait()

    rim_low = (sublane == 0) & is_source
    rim_high = (sublane == 7) & is_source
    groups = BLOCK // 4

    def ahead(level, b, slot):
        w = b * BLOCK
        value = field[level, pl.ds(REACH + w, BLOCK)].reshape(BLOCK * height, lanes)
        return y_and_z(value, zmat, ymat, None, None)

    def one_step(k, carry):
        old = lax.rem(k, 2)
        new = 1 - old
        slot = lax.rem(k, 2)
        wait_copy(k, slot)
        start_copy(k + 1, 1 - slot)

        @pl.when(k >= 2)
        def _():
            for copy in out_copies(k - 2, slot):
                copy.wait()

        first = lo_of(k) // BLOCK
        last = (hi_of(k) + BLOCK - 1) // BLOCK

        def store_ahead(values, slot):
            z, ys = values
            zbuf[slot] = z
            for g in range(groups):
                ybuf[slot, g] = ys[g]

        store_ahead(ahead(new, first, 0), lax.rem(first, 2))

        def block(b, carry):
            w = pl.multiple_of(b * BLOCK, BLOCK)
            on = active(w)
            after = jnp.minimum(b + 1, window // BLOCK - 1)
            is_own = (w >= own_lo) & (w < own_lo + thick)
            bslot = lax.rem(b, 2)

            @pl.when(on)
            def _():
                following = ahead(new, after, 0)
                for g in range(groups):
                    half = jnp.where(half_of == g % 2, 0, cols)
                    to = jnp.where(is_own, half + (w - own_lo) // 8, 2 * cols)
                    xs = [w + g * 4 + i for i in range(4)]
                    for q in range(rows8):
                        part = slice(q * 8, q * 8 + 8)
                        column_x = [
                            field[new, w + g * 4 + j, part, :] for j in range(4 + 2 * REACH)
                        ]
                        lap, dx = along_x(column_x)
                        mid = column_x[REACH : REACH + 4]
                        at = [(g * 4 + i) * height + q * 8 for i in range(4)]
                        aty = [i * height + q * 8 for i in range(4)]
                        z2 = [zbuf[bslot, p : p + 8, 0:lanes] for p in at]
                        z1 = [zbuf[bslot, p : p + 8, lanes:] for p in at]
                        y2 = [ybuf[bslot, g, p : p + 8, :] for p in aty]
                        y1 = [ybuf[bslot, g, 4 * height + p : 4 * height + p + 8, :] for p in aty]
                        lap = add(lap, scaled(1.0 / SECOND_UNIT, add(z2, y2)))
                        value = sub(
                            mul([centre[x, part, :] for x in xs], mid),
                            [field[old, REACH + x, part, :] for x in xs],
                        )
                        value = add(
                            value,
                            [
                                pulses[slot, pl.ds(pl.multiple_of(x * height + q * 8, 8), 8), :]
                                for x in xs
                            ],
                        )
                        value = add(value, mul([square[x, part, :] for x in xs], lap))
                        drift = mul([gx[x, part, :] for x in xs], dx)
                        drift = add(drift, mul([gy[x, part, :] for x in xs], y1))
                        drift = add(drift, mul([gz[x, part, :] for x in xs], z1))
                        value = sub(value, drift)
                        if q == 0:
                            low = [
                                jnp.broadcast_to(rim[k, 0, pl.ds(x, 1), :], (8, lanes)) for x in xs
                            ]
                            value = each(lambda p, v: jnp.where(rim_low, p, v), low, value)
                        if q == rows8 - 1:
                            high = [
                                jnp.broadcast_to(rim[k, 1, pl.ds(x, 1), :], (8, lanes)) for x in xs
                            ]
                            value = each(lambda p, v: jnp.where(rim_high, p, v), high, value)
                        for i in range(4):
                            field[old, REACH + xs[i], part, :] = value[i]
                            record[slot, to, i, part, :] = value[i]
                store_ahead(following, 1 - bslot)

            @pl.when(jnp.logical_not(on))
            def _():
                field[old, pl.ds(REACH + w, BLOCK)] = jnp.zeros((BLOCK, height, lanes), jnp.float32)
                for g in range(groups):
                    half = jnp.where(half_of == g % 2, 0, cols)
                    to = jnp.where(is_own, half + (w - own_lo) // 8, 2 * cols)
                    record[slot, to] = jnp.zeros((4, height, lanes), jnp.float32)
                store_ahead(ahead(new, after, 0), 1 - bslot)

            return carry

        lax.fori_loop(first, last, block, 0)
        for copy in out_copies(k, slot):
            copy.start()
        return carry

    lax.fori_loop(0, steps, one_step, 0)
    for k in (steps - 2, steps - 1):
        for copy in out_copies(k, k % 2):
            copy.wait()


def image_kernel(owners, columns, stored, meta, owner_map, prints, keep, got, *refs):
    outs, total = refs[:owners], refs[owners]
    steps, cols, half, height, lanes = keep.shape
    brick_y = outs[0].shape[2]
    for c in range(cols):
        for i in range(half):

            def one(k, value, c=c, i=i):
                return value + keep[k, c, i] * got[k, c, i]

            total[c, i] = lax.fori_loop(0, steps, one, jnp.zeros((height, lanes), jnp.float32), unroll=4)
    for b in range(owners):
        base = ((meta[0] ^ b) * columns + meta[1]) * stored

        def take(m, local, rank, b=b):
            y = pl.multiple_of((m % KY) * brick_y, brick_y)
            for i in range(half):
                outs[b][rank, i] = total[m // KY, i, pl.ds(y, brick_y), :]

        serve(prints, owner_map, base, stored, take)


def sum_kernel(owners, columns, meta, owner_map, *refs):
    prints, blocks, out = refs[:owners], refs[owners : 2 * owners], refs[2 * owners]
    stored = out.shape[0]
    base = (meta[0] * columns + meta[1]) * stored
    out[...] = jnp.zeros_like(out)
    for b in range(owners):

        def take(m, local, rank, b=b):
            out[local] += blocks[b][rank]

        serve(prints[b], owner_map, base, stored, take)


def call(kernel, out_shape, in_specs, out_specs, scratch=(), mib=8, cost=None):
    return pl.pallas_call(
        kernel,
        out_shape=out_shape,
        in_specs=in_specs,
        out_specs=out_specs,
        scratch_shapes=list(scratch),
        compiler_params=pltpu.CompilerParams(vmem_limit_bytes=mib * MIB),
        cost_estimate=cost,
    )


def run_steps(shape, meta, owner_map, inject, prints, mine, theirs, states, rims):
    f32 = jnp.float32
    owners, columns, stored, sides, _ = shape
    count = len(states)
    steps = rims[0].shape[0]
    thick, height, lanes = states[0].shape[1:]
    cols = thick // 8
    window = count * thick
    kept = jax.ShapeDtypeStruct((steps, cols, 4, height, lanes), f32)
    grid = (window, height, lanes)
    padded = (window + 2 * REACH, height, lanes)
    bricks = [x for slab in mine for x in slab] + [x for slab in theirs for x in slab]
    return call(
        functools.partial(steps_kernel, shape),
        [kept, kept],
        [smem, smem, vmem, vmem, anywhere, anywhere]
        + [smem] * len(prints)
        + [vmem] * len(bricks)
        + [anywhere] * (2 * count),
        [anywhere, anywhere],
        [
            pltpu.VMEM((2,) + padded, f32),
            pltpu.VMEM(padded, f32),
            pltpu.VMEM(grid, f32),
            pltpu.VMEM(grid, f32),
            pltpu.VMEM(grid, f32),
            pltpu.VMEM(grid, f32),
            pltpu.VMEM(grid, f32),
            pltpu.VMEM((2, window * height, lanes), f32),
            pltpu.VMEM((2, BLOCK * height, 2 * lanes), f32),
            pltpu.VMEM((2, BLOCK // 4, 8 * height, lanes), f32),
            pltpu.VMEM((2, 2 * cols + 1, 4, height, lanes), f32),
            pltpu.VMEM((steps, 2, window, lanes), f32),
            pltpu.SemaphoreType.DMA((2,)),
            pltpu.SemaphoreType.DMA((2, 2)),
            pltpu.SemaphoreType.DMA((count, 3)),
        ],
        mib=12 + window // 4,
    )(
        meta, owner_map, z_matrix(lanes), y_matrix(height, 4), *inject, *prints, *bricks, *states, *rims
    )


def injection(window, offset, early, late, height, lanes, is_source, source_cell, receivers, pulses, recorded):
    steps, spots = recorded.shape
    none = jnp.full((spots - 1,), -1, jnp.int32)
    cells = jnp.where(is_source, jnp.concatenate([source_cell, none]), receivers)
    source_values = jnp.concatenate([-pulses[:, None], jnp.zeros((steps, spots - 1), jnp.float32)], axis=1)
    values = jnp.where(is_source, source_values, recorded)
    z = cells % lanes
    rows = cells // lanes - offset * height
    rows = jnp.where(cells >= 0, rows, -1)
    every = lax.broadcasted_iota(jnp.int32, (window * height, spots), 0)
    which_row = (every == rows[None, :]).astype(jnp.bfloat16)
    which_lane = (z[:, None] == lax.broadcasted_iota(jnp.int32, (spots, lanes), 1)).astype(jnp.float32)
    high = lax.reduce_precision(values, 8, 7)
    low = lax.reduce_precision(values - high, 8, 7)
    both = jnp.concatenate([high, low], axis=1)
    spread = both[:, :, None] * jnp.concatenate([which_lane, which_lane], axis=0)[None]
    spread = spread.astype(jnp.bfloat16)
    twice = jnp.concatenate([which_row, which_row], axis=1)

    def product(rows, spread):
        return jnp.einsum("rp,kpz->krz", rows, spread, preferred_element_type=jnp.float32)

    lo, hi = late
    return (
        product(twice, spread[:early]),
        product(twice[lo * height : hi * height], spread[early:]),
    )


def per_device(
    velocity,
    density,
    owner_map,
    footprint,
    aperture,
    source_cell,
    receiver_cells,
    wavelet,
    traces,
    states,
    stored_rims,
):
    f32 = jnp.float32
    owners = lax.axis_size("shot")
    columns = lax.axis_size("dom")
    column = lax.axis_index("dom")
    pair = lax.axis_index("pair")
    shot = lax.axis_index("shot")
    stored, brick_x, brick_y, lanes = velocity.shape
    half_x = brick_x // 2
    slots = footprint.shape[1]
    per_owner = slots // owners
    thick = slots // KY * brick_x
    height = KY * brick_y
    steps = wavelet.shape[1]
    sides = columns == 2
    meta = jnp.stack(
        [shot.astype(jnp.int32), column.astype(jnp.int32), pair.astype(jnp.int32), aperture[0] * brick_x]
    )

    prints = [footprint] + [xor_swap(footprint, "shot", b) for b in range(1, owners)]
    brick = jax.ShapeDtypeStruct((per_owner, brick_x, brick_y, lanes), f32)
    packed = call(
        functools.partial(pack_kernel, owners, columns, False),
        [brick] * (owners + 1),
        [smem] * (2 + owners) + [anywhere] * 2,
        [anywhere] * (owners + 1),
        [pltpu.SemaphoreType.DMA((owners + 1, per_owner))],
    )(meta, owner_map, *prints, velocity, density)
    got = [packed[0]] + [xor_swap(packed[b], "shot", b) for b in range(1, owners)]
    if sides:
        relay = xor_swap(jnp.where(pair == 0, velocity, density), "dom", 1)
        other_prints = xor_swap(jnp.concatenate(prints, axis=0), "dom", 1)
        other_prints = [other_prints[b : b + 1] for b in range(owners)]
        relayed = call(
            functools.partial(pack_kernel, owners, columns, True),
            [brick] * owners,
            [smem] * (2 + owners) + [anywhere],
            [anywhere] * owners,
            [pltpu.SemaphoreType.DMA((owners, per_owner))],
        )(meta, owner_map, *other_prints, relay)
        far = [relayed[0]] + [xor_swap(relayed[b], "shot", b) for b in range(1, owners)]
        mine = [got, far]
        theirs = [
            [packed[owners]] + [xor_swap(x, "pair", 1) for x in got[1:]],
            [xor_swap(x, "pair", 1) for x in far],
        ]
        shown = [prints[0], other_prints[0]]
        own_lo = column * thick
        offset = 0
        window = 2 * thick
        late = (0, window)
    else:
        table = call(
            functools.partial(unpack_kernel, owners, columns, stored),
            jax.ShapeDtypeStruct((slots, brick_x, brick_y, lanes), f32),
            [smem] * 3 + [vmem] * owners,
            vmem,
        )(meta, owner_map, prints[0], *got)
        mine = [[slab] for slab in slabs_of(table)]
        theirs = [[xor_swap(slab[0], "pair", 1)] for slab in mine]
        shown = []
        offset = (column - HOPS) * thick
        window = (2 * HOPS + 1) * thick
        deep = REACH * (steps - 1 - steps // 2)
        late = (HOPS * thick - deep, (HOPS + 1) * thick + deep)

    state_slabs = slabs_of(states[0, 0])
    rim_slabs = slabs_of(stored_rims[0], first_only=True)
    inject = injection(
        window, offset, steps // 2, late, height, lanes, pair == 0,
        source_cell, receiver_cells[0], wavelet[0], traces[0],
    )
    keep, send = run_steps(
        (owners, columns, stored, sides, late[0] * height),
        meta, owner_map, inject, shown, mine, theirs, state_slabs, rim_slabs,
    )
    partner = xor_swap(send, "pair", 1)

    part = jax.ShapeDtypeStruct((per_owner, half_x, brick_y, lanes), f32)
    images = call(
        functools.partial(image_kernel, owners, columns, stored),
        [part] * owners,
        [smem] * 3 + [vmem] * 2,
        [vmem] * owners,
        [pltpu.VMEM(keep.shape[1:], f32)],
        mib=16,
    )(meta, owner_map, prints[0], keep, partner)
    returned = [images[0]] + [xor_swap(images[b], "shot", b) for b in range(1, owners)]
    return call(
        functools.partial(sum_kernel, owners, columns),
        jax.ShapeDtypeStruct((stored, half_x, brick_y, lanes), f32),
        [smem] * (2 + owners) + [vmem] * owners,
        vmem,
    )(meta, owner_map, *prints, *returned)


def solution(mesh):
    placed = (
        P(("groups", "shot", "dom"), None, None, None),
        P(("groups", "shot", "dom"), None, None, None),
        P("groups"),
        P(("groups", "shot"), "dom"),
        P(("groups", "shot")),
        P(("groups", "shot")),
        P(("groups", "shot"), None),
        P(("groups", "shot"), None),
        P(("groups", "shot"), None, None),
        P(("groups", "shot"), "pair", None, "dom", None, None),
        P(("groups", "shot"), None, None, "dom", None),
    )
    return jax.shard_map(
        per_device,
        mesh=mesh,
        in_specs=placed,
        out_specs=P(("groups", "shot", "dom"), "pair", None, None),
        check_vma=False,
    )
```

```python
import functools

import jax
import jax.numpy as jnp
import numpy as np
from jax import lax
from jax.experimental import pallas as pl
from jax.experimental.pallas import tpu as pltpu
from jax.sharding import PartitionSpec as P

KY = 4
REACH = 4

first_weights = (0.8, -0.2, 4.0 / 105.0, -1.0 / 280.0)
second_weights = (-205.0 / 72.0, 1.6, -0.2, 8.0 / 315.0, -1.0 / 560.0)

FIRST = first_weights[0]
SECOND = second_weights[1]
first_ratio = tuple(w / FIRST for w in first_weights)
second_ratio = tuple(w / SECOND for w in second_weights[1:])

SECOND_UNIT = 8064.0
FIRST_UNIT = 672.0
second_whole = (8064.0, -1008.0, 128.0, -9.0)
first_whole = (672.0, -168.0, 32.0, -3.0)

HOPS = 2
META = 4
MIB = 1024 * 1024

smem = pl.BlockSpec(memory_space=pltpu.SMEM)
vmem = pl.BlockSpec(memory_space=pltpu.VMEM)
anywhere = pl.BlockSpec(memory_space=pl.ANY)


def z_matrix(size):
    second = np.zeros((size, size))
    first = np.zeros((size, size))
    for r in range(1, REACH + 1):
        for z in range(size):
            if z + r < size:
                second[z + r, z] = second_whole[r - 1]
                first[z + r, z] = first_whole[r - 1]
            if z - r >= 0:
                second[z - r, z] = second_whole[r - 1]
                first[z - r, z] = -first_whole[r - 1]
    whole = np.concatenate([second, first], axis=1)
    return np.concatenate([whole, whole], axis=0).astype(jnp.bfloat16)


def y_matrix(across, layers):
    second = np.zeros((across, across))
    first = np.zeros((across, across))
    for r in range(1, REACH + 1):
        for y in range(across):
            if y + r < across:
                second[y, y + r] = second_whole[r - 1]
                first[y, y + r] = first_whole[r - 1]
            if y - r >= 0:
                second[y, y - r] = second_whole[r - 1]
                first[y, y - r] = -first_whole[r - 1]
    same = np.eye(layers)
    whole = np.concatenate([np.kron(same, second), np.kron(same, first)], axis=0)
    return np.concatenate([whole, whole], axis=1).astype(jnp.bfloat16)


def xor_swap(block, axis, bits):
    size = lax.axis_size(axis)
    return lax.ppermute(block, axis, [(i, i ^ bits) for i in range(size)])


def slabs_of(block, first_only=False):
    size = lax.axis_size("dom")
    pairs = lax.axis_size("pair")

    def shift(x, moves):
        if first_only:
            return lax.ppermute(x, ("dom", "pair"), [(i * pairs, j * pairs) for i, j in moves])
        return lax.ppermute(x, "dom", moves)

    if size == 1:
        return [block]
    if size == 2:
        return [block, shift(block, [(0, 1), (1, 0)])]
    up = [(i, i + 1) for i in range(size - 1)]
    down = [(i + 1, i) for i in range(size - 1)]
    found = [block]
    left = right = block
    for _ in range(HOPS):
        left = shift(left, up)
        right = shift(right, down)
        found = [left] + found + [right]
    return found


def serve(info, bricks, slots, wanted, stored, take):
    def one(m, counts):
        after = []
        for b, (at, base) in enumerate(wanted):
            local = info[META + info[META + bricks + at * slots + m]] - base
            mine = (local >= 0) & (local < stored)

            @pl.when(mine)
            def _(b=b, local=local):
                take(b, m, local, counts[b])

            after.append(counts[b] + mine.astype(jnp.int32))
        return tuple(after)

    lax.fori_loop(0, slots, one, (jnp.int32(0),) * len(wanted))


def pack_kernel(owners, columns, tables, info, table, *refs):
    outs, sems = refs[:-1], refs[-1]
    stored = table.shape[0]
    per_owner = outs[0].shape[0]
    base = (info[0] * columns + info[1]) * stored

    def take(b, m, local, rank):
        pltpu.make_async_copy(table.at[local], outs[b].at[rank], sems.at[b, rank]).start()

    serve(info, *tables, [(b, base) for b in range(owners)], stored, take)
    for b, out in enumerate(outs):
        for rank in range(per_owner):
            pltpu.make_async_copy(table.at[0], out.at[rank], sems.at[b, rank]).wait()


def unpack_kernel(owners, columns, tables, stored, info, *refs):
    blocks, out = refs[:-1], refs[-1]

    def take(b, m, local, rank):
        out[m] = blocks[b][rank]

    serve(info, *tables, sources(owners, columns, stored, info), stored, take)


def sources(owners, columns, stored, info):
    return [(0, ((info[0] ^ b) * columns + info[1]) * stored) for b in range(owners)]


def each(f, *lists):
    return [f(*items) for items in zip(*lists)]


def add(a, b):
    return each(lambda p, q: p + q, a, b)


def sub(a, b):
    return each(lambda p, q: p - q, a, b)


def mul(a, b):
    return each(lambda p, q: p * q, a, b)


def scaled(factor, a):
    return [factor * p for p in a]


def along_x(column):
    size = len(column) - 2 * REACH
    lap = slope = None
    for r in range(1, REACH + 1):
        ahead = column[REACH + r : REACH + r + size]
        behind = column[REACH - r : REACH - r + size]
        total, apart = add(ahead, behind), sub(ahead, behind)
        if r == 1:
            lap, slope = total, apart
        else:
            lap = add(lap, scaled(second_ratio[r - 1], total))
            slope = add(slope, scaled(first_ratio[r - 1], apart))
    return lap, slope


def z_slopes(high, low, zmat):
    both = jnp.concatenate([high, low], axis=1)
    return jnp.dot(both, zmat[...], preferred_element_type=jnp.float32)


def y_slopes(high, low, ymat):
    both = jnp.concatenate([high, low], axis=0)
    return jnp.dot(ymat[...], both, preferred_element_type=jnp.float32)


BLOCK = 16


def make_coefficients(
    mine, theirs, places, active, is_source, zmat, ymat, field, logs, square, centre, gx, gy, gz
):
    window, height, lanes = square.shape
    rows8 = height // 8
    zero = jnp.zeros((REACH, height, lanes), jnp.float32)
    for level in range(2):
        field[level, 0:REACH] = zero
        field[level, REACH + window : 2 * REACH + window] = zero
    logs[0:REACH] = zero
    logs[REACH + window : 2 * REACH + window] = zero

    for s in range(len(mine)):

        def fill(m, carry, s=s):
            x0 = places[s] + (m // KY) * 8
            y0 = pl.multiple_of((m % KY) * 8, 8)
            on = active(x0)
            for i in range(8):
                a = mine[s][m, i]
                b = theirs[s][m, i]
                courant = jnp.where(is_source, a, b)
                density = jnp.where(is_source, b, a)
                squared = jnp.where(on, courant * courant, 0.0)
                square[x0 + i, pl.ds(y0, 8), :] = SECOND * squared
                centre[x0 + i, pl.ds(y0, 8), :] = 2.0 + (3.0 * second_weights[0]) * squared
                logs[REACH + x0 + i, pl.ds(y0, 8), :] = jnp.where(
                    on, jnp.log(jnp.where(on, density, 1.0)), 0.0
                )
            return carry

        lax.fori_loop(0, mine[s].shape[0], fill, 0)

    def bend(b, carry):
        w = pl.multiple_of(b * BLOCK, BLOCK)
        value = logs[pl.ds(REACH + w, BLOCK)].reshape(BLOCK * height, lanes)
        high = value.astype(jnp.bfloat16)
        low = (value - high.astype(jnp.float32)).astype(jnp.bfloat16)
        z = z_slopes(high, low, zmat)
        for g in range(BLOCK // 4):
            n = 4 * height
            y = y_slopes(high[g * n : g * n + n], low[g * n : g * n + n], ymat)
            for q in range(rows8):
                part = slice(q * 8, q * 8 + 8)
                _, slope = along_x([logs[w + 4 * g + j, part, :] for j in range(4 + 2 * REACH)])
                for i in range(4):
                    x = w + 4 * g + i
                    at = i * height + q * 8
                    scale = (FIRST * FIRST / SECOND) * square[x, part, :]
                    whole = scale * (1.0 / (FIRST_UNIT * FIRST_UNIT))
                    gx[x, part, :] = scale * slope[i]
                    gy[x, part, :] = whole * y[n + at : n + at + 8]
                    gz[x, part, :] = whole * z[g * n + at : g * n + at + 8, lanes:]
        return carry

    lax.fori_loop(0, window // BLOCK, bend, 0)


def steps_kernel(sides, span, pulses_of, meta, zmat, ymat, *refs):
    begin, end, steps = span
    fresh = begin == 0
    count = 2 if sides else 2 * HOPS + 1
    injects, refs = refs[: len(pulses_of)], refs[len(pulses_of) :]
    rims, refs = refs[:count], refs[count:]
    if fresh:
        mine, theirs, refs = refs[:count], refs[count : 2 * count], refs[2 * count :]
        levels, refs = refs[:count], refs[count:]
        keep, send, field, square, centre, gx, gy, gz, logs, *refs = refs
    else:
        carried, square, centre, gx, gy, gz, keep, send, field, *refs = refs
    pulses, zbuf, ybuf, record, rim, sems, out_sems, in_sems = refs
    thick, lanes = rims[0].shape[2:]
    window, height = square.shape[:2]
    cols = thick // 8
    rows8 = height // 8
    column = meta[1]
    is_source = meta[2] == 0
    limit = meta[3]
    half_of = meta[2]
    sublane = lax.broadcasted_iota(jnp.int32, (8, lanes), 0)
    if sides:
        own_lo = column * thick
        places = [column * thick, (1 - column) * thick]
    else:
        own_lo = HOPS * thick
        places = [s * thick for s in range(count)]

    def active(w):
        x = w if sides else w + column * thick - own_lo
        return (x >= 0) & (x < limit)

    def lo_of(k):
        return jnp.maximum(0, own_lo - REACH * (steps - 1 - k))

    def hi_of(k):
        return jnp.minimum(window, own_lo + thick + REACH * (steps - 1 - k))

    def pulse_copies(k, slot, act):
        for inject, (k_lo, k_hi, row_lo) in zip(injects, pulses_of):

            @pl.when((k >= k_lo) & (k < k_hi))
            def _(inject=inject, k_lo=k_lo, row_lo=row_lo):
                there = pulses.at[slot, pl.ds(row_lo, inject.shape[1])]
                act(pltpu.make_async_copy(inject.at[k - k_lo], there, sems.at[slot]))

    def out_copies(k, slot):
        return [
            pltpu.make_async_copy(
                record.at[slot, pl.ds(0, cols)], keep.at[k - begin], out_sems.at[slot, 0]
            ),
            pltpu.make_async_copy(
                record.at[slot, pl.ds(cols, cols)], send.at[k - begin], out_sems.at[slot, 1]
            ),
        ]

    def in_copies(s):
        place = places[s] if isinstance(places[s], int) else pl.multiple_of(places[s], 8)
        copies = [
            pltpu.make_async_copy(
                rims[s].at[pl.ds(begin, end - begin)],
                rim.at[:, :, pl.ds(place, thick), :],
                in_sems.at[s, 2],
            )
        ]
        if fresh:
            copies += [
                pltpu.make_async_copy(
                    levels[s].at[level],
                    field.at[level, pl.ds(REACH + place, thick)],
                    in_sems.at[s, level],
                )
                for level in range(2)
            ]
        return copies

    pulse_copies(begin, 0, lambda copy: copy.start())
    for s in range(count):
        for copy in in_copies(s):
            copy.start()

    if fresh:
        make_coefficients(
            mine, theirs, places, active, is_source, zmat, ymat, field, logs, square, centre, gx, gy, gz
        )
    else:

        def bring(w, carry):
            for level in range(2):
                field[level, w] = carried[level, w]
            return carry

        lax.fori_loop(0, window + 2 * REACH, bring, 0, unroll=4)
    for s in range(count):
        for copy in in_copies(s):
            copy.wait()

    rim_low = (sublane == 0) & is_source
    rim_high = (sublane == 7) & is_source
    groups = BLOCK // 4

    def cut(level, b, at, size):
        w = b * BLOCK + at
        value = field[level, pl.ds(REACH + w, size)].reshape(size * height, lanes)
        high = value.astype(jnp.bfloat16)
        return high, (value - high.astype(jnp.float32)).astype(jnp.bfloat16)

    def store_ahead(level, b, slot):
        high, low = cut(level, b, 0, BLOCK)
        zbuf[slot] = z_slopes(high, low, zmat)
        n = 4 * height
        for g in range(groups):
            ybuf[slot, g] = y_slopes(high[g * n : g * n + n], low[g * n : g * n + n], ymat)

    def one_step(k, buf):
        old = lax.rem(k, 2)
        new = 1 - old
        slot = lax.rem(k, 2)
        pulse_copies(k, slot, lambda copy: copy.wait())
        pulse_copies(k + 1, 1 - slot, lambda copy: copy.start())

        @pl.when(k >= begin + 2)
        def _():
            for copy in out_copies(k - 2, slot):
                copy.wait()

        first = lo_of(k) // BLOCK
        last = (hi_of(k) + BLOCK - 1) // BLOCK

        first_next = lo_of(k + 1) // BLOCK

        def block(b, bslot):
            w = pl.multiple_of(b * BLOCK, BLOCK)
            on = active(w) | active(w + BLOCK - 8)
            at_end = b == last - 1
            after = jnp.where(at_end, first_next, b + 1)
            level = jnp.where(at_end, old, new)
            is_own = (w >= own_lo) & (w < own_lo + thick)

            @pl.when(on)
            def _():
                top, rest = cut(level, after, 0, BLOCK)
                n = 4 * height
                for g in range(groups):
                    following_y = y_slopes(top[g * n : g * n + n], rest[g * n : g * n + n], ymat)
                    half = jnp.where(half_of == g % 2, 0, cols)
                    to = jnp.where(is_own, half + (w - own_lo) // 8 + g // 2, 2 * cols)
                    xs = [w + g * 4 + i for i in range(4)]
                    for q in range(rows8):
                        part = slice(q * 8, q * 8 + 8)
                        column_x = [
                            field[new, w + g * 4 + j, part, :] for j in range(4 + 2 * REACH)
                        ]
                        lap, dx = along_x(column_x)
                        mid = column_x[REACH : REACH + 4]
                        at = [(g * 4 + i) * height + q * 8 for i in range(4)]
                        aty = [i * height + q * 8 for i in range(4)]
                        z2 = [zbuf[bslot, p : p + 8, 0:lanes] for p in at]
                        z1 = [zbuf[bslot, p : p + 8, lanes:] for p in at]
                        y2 = [ybuf[bslot, g, p : p + 8, :] for p in aty]
                        y1 = [ybuf[bslot, g, 4 * height + p : 4 * height + p + 8, :] for p in aty]
                        lap = add(lap, scaled(1.0 / SECOND_UNIT, add(z2, y2)))
                        value = sub(
                            mul([centre[x, part, :] for x in xs], mid),
                            [field[old, REACH + x, part, :] for x in xs],
                        )
                        value = add(
                            value,
                            [
                                pulses[slot, pl.ds(pl.multiple_of(x * height + q * 8, 8), 8), :]
                                for x in xs
                            ],
                        )
                        value = add(value, mul([square[x, part, :] for x in xs], lap))
                        drift = mul([gx[x, part, :] for x in xs], dx)
                        drift = add(drift, mul([gy[x, part, :] for x in xs], y1))
                        drift = add(drift, mul([gz[x, part, :] for x in xs], z1))
                        value = sub(value, drift)
                        if q == 0:
                            low = [
                                jnp.broadcast_to(rim[k - begin, 0, pl.ds(x, 1), :], (8, lanes)) for x in xs
                            ]
                            value = each(lambda p, v: jnp.where(rim_low, p, v), low, value)
                        if q == rows8 - 1:
                            high = [
                                jnp.broadcast_to(rim[k - begin, 1, pl.ds(x, 1), :], (8, lanes)) for x in xs
                            ]
                            value = each(lambda p, v: jnp.where(rim_high, p, v), high, value)
                        for i in range(4):
                            field[old, REACH + xs[i], part, :] = value[i]
                            record[slot, to, i, part, :] = value[i]
                    ybuf[1 - bslot, g] = following_y
                zbuf[1 - bslot] = z_slopes(top, rest, zmat)

            for half in range(BLOCK // 8):
                x8 = w + half * 8

                @pl.when(on & jnp.logical_not(active(x8)))
                def _(x8=x8, half=half):
                    field[old, pl.ds(REACH + x8, 8)] = jnp.zeros((8, height, lanes), jnp.float32)
                    for g in range(2):
                        to = jnp.where(is_own, jnp.where(half_of == g, 0, cols) + (x8 - own_lo) // 8, 2 * cols)
                        record[slot, to] = jnp.zeros((4, height, lanes), jnp.float32)

            @pl.when(jnp.logical_not(on))
            def _():
                field[old, pl.ds(REACH + w, BLOCK)] = jnp.zeros((BLOCK, height, lanes), jnp.float32)
                for g in range(groups):
                    half = jnp.where(half_of == g % 2, 0, cols)
                    to = jnp.where(is_own, half + (w - own_lo) // 8 + g // 2, 2 * cols)
                    record[slot, to] = jnp.zeros((4, height, lanes), jnp.float32)
                store_ahead(level, after, 1 - bslot)

            return 1 - bslot

        buf = lax.fori_loop(first, last, block, buf)
        for copy in out_copies(k, slot):
            copy.start()
        return buf

    store_ahead(1 - begin % 2, lo_of(begin) // BLOCK, 0)
    lax.fori_loop(begin, end, one_step, 0)
    for k in (end - 2, end - 1):
        for copy in out_copies(k, k % 2):
            copy.wait()


def multiply(keep, got, start, total):
    steps, cols, half, height, lanes = keep.shape
    for c in range(cols):
        for i in range(half):

            def one(k, value, c=c, i=i):
                return value + keep[k, c, i] * got[k, c, i]

            first = start[c, i] if start is not None else jnp.zeros((height, lanes), jnp.float32)
            total[c, i] = lax.fori_loop(0, steps, one, first, unroll=4)


def multiply_kernel(keep, got, total):
    multiply(keep, got, None, total)


def image_kernel(owners, columns, tables, stored, info, before, keep, got, *refs):
    outs, total = refs[:owners], refs[owners]
    half = keep.shape[2]
    brick_y = outs[0].shape[2]
    multiply(keep, got, before, total)

    def take(b, m, local, rank):
        y = pl.multiple_of((m % KY) * brick_y, brick_y)
        for i in range(half):
            outs[b][rank, i] = total[m // KY, i, pl.ds(y, brick_y), :]

    serve(info, *tables, sources(owners, columns, stored, info), stored, take)


def sum_kernel(owners, columns, tables, info, *refs):
    blocks, out = refs[:-1], refs[-1]
    stored = out.shape[0]
    base = (info[0] * columns + info[1]) * stored
    out[...] = jnp.zeros_like(out)

    def take(b, m, local, rank):
        out[local] += blocks[b][rank]

    serve(info, *tables, [(b, base) for b in range(owners)], stored, take)


def call(kernel, out_shape, in_specs, out_specs, scratch=(), mib=8, flops=1):
    return pl.pallas_call(
        kernel,
        out_shape=out_shape,
        in_specs=in_specs,
        out_specs=out_specs,
        scratch_shapes=list(scratch),
        compiler_params=pltpu.CompilerParams(vmem_limit_bytes=mib * MIB),
        cost_estimate=pl.CostEstimate(flops=flops, bytes_accessed=1, transcendentals=0),
    )


def run_steps(sides, span, pulses_of, shape, meta, injects, rims, inputs):
    f32 = jnp.float32
    begin, end, steps = span
    window, height, lanes = shape
    count = len(rims)
    thick = window // count
    cols = thick // 8
    fresh = begin == 0
    kept = jax.ShapeDtypeStruct((end - begin, cols, 4, height, lanes), f32)
    padded = (window + 2 * REACH, height, lanes)
    outs, specs, scratch = [kept, kept], [anywhere, anywhere], []
    if fresh:
        if end < steps:
            outs += [jax.ShapeDtypeStruct((2,) + padded, f32)] + [jax.ShapeDtypeStruct(shape, f32)] * 5
            specs += [vmem] * 6
        else:
            scratch = [pltpu.VMEM((2,) + padded, f32)] + [pltpu.VMEM(shape, f32)] * 5
        scratch += [pltpu.VMEM(padded, f32)]
        in_specs = [vmem] * (2 * count) + [anywhere] * count
    else:
        scratch = [pltpu.VMEM((2,) + padded, f32)]
        in_specs = [vmem] * 6
    return call(
        functools.partial(steps_kernel, sides, span, pulses_of),
        outs,
        [smem, vmem, vmem] + [anywhere] * (len(injects) + count) + in_specs,
        specs,
        scratch
        + [
            pltpu.VMEM((2, window * height, lanes), f32),
            pltpu.VMEM((2, BLOCK * height, 2 * lanes), f32),
            pltpu.VMEM((2, BLOCK // 4, 8 * height, lanes), f32),
            pltpu.VMEM((2, 2 * cols + 1, 4, height, lanes), f32),
            pltpu.VMEM((end - begin, 2, window, lanes), f32),
            pltpu.SemaphoreType.DMA((2,)),
            pltpu.SemaphoreType.DMA((2, 2)),
            pltpu.SemaphoreType.DMA((count, 3)),
        ],
        mib=12 + window // 4,
        flops=(end - begin) * window * height * lanes * 2048,
    )(meta, z_matrix(lanes), y_matrix(height, 4), *injects, *rims, *inputs)


def injection(window, offset, split, late, height, lanes, is_source, source_cell, receivers, pulses, recorded):
    steps, spots = recorded.shape
    none = jnp.full((spots - 1,), -1, jnp.int32)
    cells = jnp.where(is_source, jnp.concatenate([source_cell, none]), receivers)
    source_values = jnp.concatenate([-pulses[:, None], jnp.zeros((steps, spots - 1), jnp.float32)], axis=1)
    values = jnp.where(is_source, source_values, recorded)
    z = cells % lanes
    rows = cells // lanes - offset * height
    rows = jnp.where(cells >= 0, rows, -1)
    every = lax.broadcasted_iota(jnp.int32, (window * height, spots), 0)
    which_row = (every == rows[None, :]).astype(jnp.bfloat16)
    which_lane = (z[:, None] == lax.broadcasted_iota(jnp.int32, (spots, lanes), 1)).astype(jnp.float32)
    high = lax.reduce_precision(values, 8, 7)
    low = lax.reduce_precision(values - high, 8, 7)
    both = jnp.concatenate([high, low], axis=1)
    spread = both[:, :, None] * jnp.concatenate([which_lane, which_lane], axis=0)[None]
    spread = spread.astype(jnp.bfloat16)
    twice = jnp.concatenate([which_row, which_row], axis=1)

    def product(rows, spread):
        return jnp.einsum("rp,kpz->krz", rows, spread, preferred_element_type=jnp.float32)

    lo, hi = late
    return (
        product(twice, spread[:split]),
        product(twice[lo * height : hi * height], spread[split:]),
    )


def per_device(
    velocity,
    density,
    owner_map,
    footprint,
    aperture,
    source_cell,
    receiver_cells,
    wavelet,
    traces,
    states,
    stored_rims,
):
    f32 = jnp.float32
    owners = lax.axis_size("shot")
    columns = lax.axis_size("dom")
    column = lax.axis_index("dom")
    pair = lax.axis_index("pair")
    shot = lax.axis_index("shot")
    stored, brick_x, brick_y, lanes = velocity.shape
    half_x = brick_x // 2
    slots = footprint.shape[1]
    per_owner = slots // owners
    thick = slots // KY * brick_x
    height = KY * brick_y
    steps = wavelet.shape[1]
    sides = columns == 2
    meta = jnp.stack(
        [shot.astype(jnp.int32), column.astype(jnp.int32), pair.astype(jnp.int32), aperture[0] * brick_x]
    )
    tables = (owner_map.shape[0], slots)

    table = jnp.where(pair == 0, velocity, density)
    prints = [footprint[0]] + [xor_swap(footprint[0], "shot", b) for b in range(1, owners)]
    info = jnp.concatenate([meta, owner_map, *prints])
    split = 12 if sides else 8
    if sides:
        offset = 0
        window = 2 * thick
        late = (0, window)
    else:
        offset = (column - HOPS) * thick
        window = (2 * HOPS + 1) * thick
        deep = REACH * (steps - 1 - split)
        late = (HOPS * thick - deep, (HOPS + 1) * thick + deep)
    early_inject, late_inject = injection(
        window, offset, split, late, height, lanes, pair == 0,
        source_cell, receiver_cells[0], wavelet[0], traces[0],
    )
    brick = jax.ShapeDtypeStruct((per_owner, brick_x, brick_y, lanes), f32)

    fields = slabs_of(states[0, 0])
    packed = call(
        functools.partial(pack_kernel, owners, columns, tables),
        [brick] * owners,
        [smem, anywhere],
        [anywhere] * owners,
        [pltpu.SemaphoreType.DMA((owners, per_owner))],
    )(info, table)
    got = [packed[0]] + [xor_swap(packed[b], "shot", b) for b in range(1, owners)]
    bricks = call(
        functools.partial(unpack_kernel, owners, columns, tables, stored),
        jax.ShapeDtypeStruct((slots, brick_x, brick_y, lanes), f32),
        [smem] + [vmem] * owners,
        vmem,
    )(info, *got)
    mine = slabs_of(bricks)
    shape = (window, height, lanes)
    if sides:
        rims_here, _ = lax.optimization_barrier((stored_rims[0], info))
        rim_slabs = slabs_of(rims_here, first_only=True)
        mine[1], early_inject, late_inject, rim_slabs[1] = lax.optimization_barrier(
            (mine[1], early_inject, late_inject, rim_slabs[1])
        )
        theirs = [xor_swap(slab, "pair", 1) for slab in mine]
        keep, send, *carried = run_steps(
            sides, (0, split, steps), [(0, split, 0)], shape, meta, [early_inject], rim_slabs,
            [*mine, *theirs, *fields],
        )
        partner = xor_swap(send, "pair", 1)
        keep_last, send_last = run_steps(
            sides, (split, steps, steps), [(split, steps, 0)], shape, meta, [late_inject], rim_slabs,
            carried,
        )
        total = call(
            multiply_kernel, jax.ShapeDtypeStruct(keep.shape[1:], f32), [vmem] * 2, vmem, mib=16
        )(keep, partner)
    else:
        theirs = [xor_swap(slab, "pair", 1) for slab in mine]
        keep_last, send_last = run_steps(
            sides, (0, steps, steps), [(0, split, 0), (split, steps, late[0] * height)], shape, meta,
            [early_inject, late_inject], slabs_of(stored_rims[0], first_only=True),
            [*mine, *theirs, *fields],
        )
        total = jnp.zeros(keep_last.shape[1:], f32)
    partner_last = xor_swap(send_last, "pair", 1)

    part = jax.ShapeDtypeStruct((per_owner, half_x, brick_y, lanes), f32)
    images = call(
        functools.partial(image_kernel, owners, columns, tables, stored),
        [part] * owners,
        [smem] + [vmem] * 3,
        [vmem] * owners,
        [pltpu.VMEM(total.shape, f32)],
        mib=16,
    )(info, total, keep_last, partner_last)
    returned = [images[0]] + [xor_swap(images[b], "shot", b) for b in range(1, owners)]
    return call(
        functools.partial(sum_kernel, owners, columns, tables),
        jax.ShapeDtypeStruct((stored, half_x, brick_y, lanes), f32),
        [smem] + [vmem] * owners,
        vmem,
    )(info, *returned)


def solution(mesh):
    placed = (
        P(("groups", "shot", "dom"), None, None, None),
        P(("groups", "shot", "dom"), None, None, None),
        P("groups"),
        P(("groups", "shot"), "dom"),
        P(("groups", "shot")),
        P(("groups", "shot")),
        P(("groups", "shot"), None),
        P(("groups", "shot"), None),
        P(("groups", "shot"), None, None),
        P(("groups", "shot"), "pair", None, "dom", None, None),
        P(("groups", "shot"), None, None, "dom", None),
    )
    return jax.shard_map(
        per_device,
        mesh=mesh,
        in_specs=placed,
        out_specs=P(("groups", "shot", "dom"), "pair", None, None),
        check_vma=False,
    )
```

```python
import functools

import jax
import jax.numpy as jnp
import numpy as np
from jax import lax
from jax.experimental import pallas as pl
from jax.experimental.pallas import tpu as pltpu
from jax.sharding import PartitionSpec as P

KY = 4
REACH = 4

first_weights = (0.8, -0.2, 4.0 / 105.0, -1.0 / 280.0)
second_weights = (-205.0 / 72.0, 1.6, -0.2, 8.0 / 315.0, -1.0 / 560.0)

FIRST = first_weights[2]
SECOND = second_weights[3]
first_ratio = (21.0, -5.25, 1.0, -0.09375)
second_ratio = (63.0, -7.875, 1.0, -0.0703125)

HOPS = 2
META = 4
MIB = 1024 * 1024

smem = pl.BlockSpec(memory_space=pltpu.SMEM)
vmem = pl.BlockSpec(memory_space=pltpu.VMEM)
anywhere = pl.BlockSpec(memory_space=pl.ANY)


def z_matrix(size):
    second = np.zeros((size, size))
    first = np.zeros((size, size))
    for r in range(1, REACH + 1):
        for z in range(size):
            if z + r < size:
                second[z + r, z] = second_ratio[r - 1]
                first[z + r, z] = first_ratio[r - 1]
            if z - r >= 0:
                second[z - r, z] = second_ratio[r - 1]
                first[z - r, z] = -first_ratio[r - 1]
    whole = np.concatenate([second, first], axis=1)
    return np.concatenate([whole, whole], axis=0).astype(jnp.bfloat16)


def y_matrix(across, layers):
    second = np.zeros((across, across))
    first = np.zeros((across, across))
    for r in range(1, REACH + 1):
        for y in range(across):
            if y + r < across:
                second[y, y + r] = second_ratio[r - 1]
                first[y, y + r] = first_ratio[r - 1]
            if y - r >= 0:
                second[y, y - r] = second_ratio[r - 1]
                first[y, y - r] = -first_ratio[r - 1]
    same = np.eye(layers)
    whole = np.concatenate([np.kron(same, second), np.kron(same, first)], axis=0)
    return np.concatenate([whole, whole], axis=1).astype(jnp.bfloat16)


def xor_swap(block, axis, bits):
    size = lax.axis_size(axis)
    return lax.ppermute(block, axis, [(i, i ^ bits) for i in range(size)])


def slabs_of(block, first_only=False):
    size = lax.axis_size("dom")
    pairs = lax.axis_size("pair")

    def shift(x, moves):
        if first_only:
            return lax.ppermute(x, ("dom", "pair"), [(i * pairs, j * pairs) for i, j in moves])
        return lax.ppermute(x, "dom", moves)

    if size == 1:
        return [block]
    if size == 2:
        return [block, shift(block, [(0, 1), (1, 0)])]
    up = [(i, i + 1) for i in range(size - 1)]
    down = [(i + 1, i) for i in range(size - 1)]
    found = [block]
    left = right = block
    for _ in range(HOPS):
        left = shift(left, up)
        right = shift(right, down)
        found = [left] + found + [right]
    return found


def serve(info, bricks, slots, wanted, stored, take):
    def one(m, counts):
        after = []
        for b, (at, base) in enumerate(wanted):
            local = info[META + info[META + bricks + at * slots + m]] - base
            mine = (local >= 0) & (local < stored)

            @pl.when(mine)
            def _(b=b, local=local):
                take(b, m, local, counts[b])

            after.append(counts[b] + mine.astype(jnp.int32))
        return tuple(after)

    lax.fori_loop(0, slots, one, (jnp.int32(0),) * len(wanted))


def pack_kernel(owners, columns, tables, info, table, *refs):
    outs, rows, sems = refs[:owners], refs[owners], refs[owners + 1]
    stored = table.shape[0]
    per_owner = outs[0].shape[0]
    base = (info[0] * columns + info[1]) * stored

    def take(b, m, local, rank):
        rows[b * per_owner + rank] = local
        pltpu.make_async_copy(table.at[local], outs[b].at[rank], sems.at[b, rank]).start()

    serve(info, *tables, [(b, base) for b in range(owners)], stored, take)
    for b, out in enumerate(outs):
        for rank in range(per_owner):
            pltpu.make_async_copy(table.at[0], out.at[rank], sems.at[b, rank]).wait()


def unpack_kernel(owners, columns, tables, stored, info, *refs):
    blocks, out, places = refs[:owners], refs[owners], refs[owners + 1]
    per_owner = blocks[0].shape[0]

    def take(b, m, local, rank):
        places[b * per_owner + rank] = m
        out[m] = blocks[b][rank]

    serve(info, *tables, sources(owners, columns, stored, info), stored, take)


def sources(owners, columns, stored, info):
    return [(0, ((info[0] ^ b) * columns + info[1]) * stored) for b in range(owners)]


def each(f, *lists):
    return [f(*items) for items in zip(*lists)]


def add(a, b):
    return each(lambda p, q: p + q, a, b)


def sub(a, b):
    return each(lambda p, q: p - q, a, b)


def mul(a, b):
    return each(lambda p, q: p * q, a, b)


def scaled(factor, a):
    return [factor * p for p in a]


def along_x(column):
    size = len(column) - 2 * REACH
    lap = slope = None
    for r in (3, 1, 2, 4):
        ahead = column[REACH + r : REACH + r + size]
        behind = column[REACH - r : REACH - r + size]
        total, apart = add(ahead, behind), sub(ahead, behind)
        if r == 3:
            lap, slope = total, apart
        else:
            lap = add(lap, scaled(second_ratio[r - 1], total))
            slope = add(slope, scaled(first_ratio[r - 1], apart))
    return lap, slope


def z_slopes(high, low, zmat):
    both = jnp.concatenate([high, low], axis=1)
    return jnp.dot(both, zmat[...], preferred_element_type=jnp.float32)


def y_slopes(high, low, ymat):
    n = ymat.shape[0] // 2
    both = [
        jnp.concatenate([high[at : at + n], low[at : at + n]], axis=0) for at in range(0, 2 * n, n)
    ]
    return jnp.dot(ymat[...], jnp.concatenate(both, axis=1), preferred_element_type=jnp.float32)


BLOCK = 16


def make_coefficients(
    mine, theirs, places, active, is_source, zmat, ymat, field, logs, square, centre, gx, gy, gz
):
    window, height, lanes = square.shape
    rows8 = height // 8
    zero = jnp.zeros((REACH, height, lanes), jnp.float32)
    for level in range(2):
        field[level, 0:REACH] = zero
        field[level, REACH + window : 2 * REACH + window] = zero
    logs[0:REACH] = zero
    logs[REACH + window : 2 * REACH + window] = zero

    for s in range(len(mine)):

        def fill(m, carry, s=s):
            x0 = places[s] + (m // KY) * 8
            y0 = pl.multiple_of((m % KY) * 8, 8)
            on = active(x0)
            for i in range(8):
                a = mine[s][m, i]
                b = theirs[s][m, i]
                courant = jnp.where(is_source, a, b)
                density = jnp.where(is_source, b, a)
                squared = jnp.where(on, courant * courant, 0.0)
                square[x0 + i, pl.ds(y0, 8), :] = SECOND * squared
                centre[x0 + i, pl.ds(y0, 8), :] = 2.0 + (3.0 * second_weights[0]) * squared
                logs[REACH + x0 + i, pl.ds(y0, 8), :] = jnp.where(
                    on, jnp.log(jnp.where(on, density, 1.0)), 0.0
                )
            return carry

        lax.fori_loop(0, mine[s].shape[0], fill, 0)

    def bend(b, carry):
        w = pl.multiple_of(b * BLOCK, BLOCK)
        value = logs[pl.ds(REACH + w, BLOCK)].reshape(BLOCK * height, lanes)
        high = value.astype(jnp.bfloat16)
        low = (value - high.astype(jnp.float32)).astype(jnp.bfloat16)
        z = z_slopes(high, low, zmat)
        n = 4 * height
        for g in range(BLOCK // 4):
            if g % 2 == 0:
                pair = slice(g * n, g * n + 2 * n)
                y = y_slopes(high[pair], low[pair], ymat)
            side = slice(g % 2 * lanes, g % 2 * lanes + lanes)
            for q in range(rows8):
                part = slice(q * 8, q * 8 + 8)
                _, slope = along_x([logs[w + 4 * g + j, part, :] for j in range(4 + 2 * REACH)])
                for i in range(4):
                    x = w + 4 * g + i
                    at = i * height + q * 8
                    scale = (FIRST * FIRST / SECOND) * square[x, part, :]
                    gx[x, part, :] = scale * slope[i]
                    gy[x, part, :] = scale * y[n + at : n + at + 8, side]
                    gz[x, part, :] = scale * z[g * n + at : g * n + at + 8, lanes:]
        return carry

    lax.fori_loop(0, window // BLOCK, bend, 0)


def steps_kernel(sides, span, pulses_of, meta, zmat, ymat, *refs):
    begin, end, steps = span
    fresh = begin == 0
    count = 2 if sides else 2 * HOPS + 1
    injects, refs = refs[: len(pulses_of)], refs[len(pulses_of) :]
    rims, refs = refs[:count], refs[count:]
    if fresh:
        mine, theirs, refs = refs[:count], refs[count : 2 * count], refs[2 * count :]
        levels, refs = refs[:count], refs[count:]
        keep, send, field, square, centre, gx, gy, gz, logs, *refs = refs
    else:
        carried, square, centre, gx, gy, gz, keep, send, field, *refs = refs
    pulses, zbuf, ybuf, record, rim, sems, out_sems, in_sems = refs
    thick, lanes = rims[0].shape[2:]
    window, height = square.shape[:2]
    cols = thick // 8
    rows8 = height // 8
    column = meta[1]
    is_source = meta[2] == 0
    limit = meta[3]
    half_of = meta[2]
    sublane = lax.broadcasted_iota(jnp.int32, (8, lanes), 0)
    if sides:
        own_lo = column * thick
        places = [column * thick, (1 - column) * thick]
    else:
        own_lo = HOPS * thick
        places = [s * thick for s in range(count)]

    def active(w):
        x = w if sides else w + column * thick - own_lo
        return (x >= 0) & (x < limit)

    def lo_of(k):
        return jnp.maximum(0, own_lo - REACH * (steps - 1 - k))

    def hi_of(k):
        return jnp.minimum(window, own_lo + thick + REACH * (steps - 1 - k))

    def pulse_copies(k, slot, act):
        for inject, (k_lo, k_hi, row_lo) in zip(injects, pulses_of):

            @pl.when((k >= k_lo) & (k < k_hi))
            def _(inject=inject, k_lo=k_lo, row_lo=row_lo):
                there = pulses.at[slot, pl.ds(row_lo, inject.shape[1])]
                act(pltpu.make_async_copy(inject.at[k - k_lo], there, sems.at[slot]))

    def out_copies(k, slot):
        return [
            pltpu.make_async_copy(
                record.at[slot, pl.ds(0, cols)], keep.at[k - begin], out_sems.at[slot, 0]
            ),
            pltpu.make_async_copy(
                record.at[slot, pl.ds(cols, cols)], send.at[k - begin], out_sems.at[slot, 1]
            ),
        ]

    def in_copies(s):
        place = places[s] if isinstance(places[s], int) else pl.multiple_of(places[s], 8)
        copies = [
            pltpu.make_async_copy(
                rims[s].at[pl.ds(begin, end - begin)],
                rim.at[:, :, pl.ds(place, thick), :],
                in_sems.at[s, 2],
            )
        ]
        if fresh:
            copies += [
                pltpu.make_async_copy(
                    levels[s].at[level],
                    field.at[level, pl.ds(REACH + place, thick)],
                    in_sems.at[s, level],
                )
                for level in range(2)
            ]
        return copies

    pulse_copies(begin, 0, lambda copy: copy.start())
    for s in range(count):
        for copy in in_copies(s):
            copy.start()

    if fresh:
        make_coefficients(
            mine, theirs, places, active, is_source, zmat, ymat, field, logs, square, centre, gx, gy, gz
        )
    else:

        def bring(w, carry):
            for level in range(2):
                field[level, w] = carried[level, w]
            return carry

        lax.fori_loop(0, window + 2 * REACH, bring, 0, unroll=4)
    for s in range(count):
        for copy in in_copies(s):
            copy.wait()

    rim_low = (sublane == 0) & is_source
    rim_high = (sublane == 7) & is_source
    groups = BLOCK // 4

    def cut(level, b, at, size):
        w = b * BLOCK + at
        value = field[level, pl.ds(REACH + w, size)].reshape(size * height, lanes)
        high = value.astype(jnp.bfloat16)
        return high, (value - high.astype(jnp.float32)).astype(jnp.bfloat16)

    def store_ahead(level, b, slot):
        high, low = cut(level, b, 0, BLOCK)
        zbuf[slot] = z_slopes(high, low, zmat)
        n = 8 * height
        for h in range(groups // 2):
            pair = slice(h * n, h * n + n)
            ybuf[slot, h] = y_slopes(high[pair], low[pair], ymat)

    def one_step(k, buf):
        old = lax.rem(k, 2)
        new = 1 - old
        slot = lax.rem(k - begin, 2)
        pulse_copies(k, slot, lambda copy: copy.wait())
        pulse_copies(k + 1, 1 - slot, lambda copy: copy.start())

        @pl.when(k >= begin + 2)
        def _():
            for copy in out_copies(k - 2, slot):
                copy.wait()

        first = lo_of(k) // BLOCK
        last = (hi_of(k) + BLOCK - 1) // BLOCK

        first_next = lo_of(k + 1) // BLOCK

        def block(b, bslot):
            w = pl.multiple_of(b * BLOCK, BLOCK)
            on = active(w) | active(w + BLOCK - 8)
            at_end = b == last - 1
            after = jnp.where(at_end, first_next, b + 1)
            level = jnp.where(at_end, old, new)
            is_own = (w >= own_lo) & (w < own_lo + thick)

            @pl.when(on)
            def _():
                top, rest = cut(level, after, 0, BLOCK)
                n = 4 * height
                for g in range(groups):
                    side = slice(g % 2 * lanes, g % 2 * lanes + lanes)
                    half = jnp.where(half_of == g % 2, 0, cols)
                    to = jnp.where(is_own, half + (w - own_lo) // 8 + g // 2, 2 * cols)
                    xs = [w + g * 4 + i for i in range(4)]
                    for q in range(rows8):
                        part = slice(q * 8, q * 8 + 8)
                        column_x = [
                            field[new, w + g * 4 + j, part, :] for j in range(4 + 2 * REACH)
                        ]
                        lap, dx = along_x(column_x)
                        mid = column_x[REACH : REACH + 4]
                        at = [(g * 4 + i) * height + q * 8 for i in range(4)]
                        aty = [i * height + q * 8 for i in range(4)]
                        z2 = [zbuf[bslot, p : p + 8, 0:lanes] for p in at]
                        z1 = [zbuf[bslot, p : p + 8, lanes:] for p in at]
                        y2 = [ybuf[bslot, g // 2, p : p + 8, side] for p in aty]
                        y1 = [ybuf[bslot, g // 2, n + p : n + p + 8, side] for p in aty]
                        lap = add(lap, add(z2, y2))
                        value = sub(
                            mul([centre[x, part, :] for x in xs], mid),
                            [field[old, REACH + x, part, :] for x in xs],
                        )
                        value = add(
                            value,
                            [
                                pulses[slot, pl.ds(pl.multiple_of(x * height + q * 8, 8), 8), :]
                                for x in xs
                            ],
                        )
                        value = add(value, mul([square[x, part, :] for x in xs], lap))
                        drift = mul([gx[x, part, :] for x in xs], dx)
                        drift = add(drift, mul([gy[x, part, :] for x in xs], y1))
                        drift = add(drift, mul([gz[x, part, :] for x in xs], z1))
                        value = sub(value, drift)
                        if q == 0:
                            low = [
                                jnp.broadcast_to(rim[k - begin, 0, pl.ds(x, 1), :], (8, lanes)) for x in xs
                            ]
                            value = each(lambda p, v: jnp.where(rim_low, p, v), low, value)
                        if q == rows8 - 1:
                            high = [
                                jnp.broadcast_to(rim[k - begin, 1, pl.ds(x, 1), :], (8, lanes)) for x in xs
                            ]
                            value = each(lambda p, v: jnp.where(rim_high, p, v), high, value)
                        for i in range(4):
                            field[old, REACH + xs[i], part, :] = value[i]
                            record[slot, to, i, part, :] = value[i]
                zbuf[1 - bslot] = z_slopes(top, rest, zmat)
                for h in range(groups // 2):
                    ybuf[1 - bslot, h] = y_slopes(top[h * 2 * n : h * 2 * n + 2 * n], rest[h * 2 * n : h * 2 * n + 2 * n], ymat)

            for half in range(BLOCK // 8):
                x8 = w + half * 8

                @pl.when(on & jnp.logical_not(active(x8)))
                def _(x8=x8, half=half):
                    field[old, pl.ds(REACH + x8, 8)] = jnp.zeros((8, height, lanes), jnp.float32)
                    for g in range(2):
                        to = jnp.where(is_own, jnp.where(half_of == g, 0, cols) + (x8 - own_lo) // 8, 2 * cols)
                        record[slot, to] = jnp.zeros((4, height, lanes), jnp.float32)

            @pl.when(jnp.logical_not(on))
            def _():
                field[old, pl.ds(REACH + w, BLOCK)] = jnp.zeros((BLOCK, height, lanes), jnp.float32)
                for g in range(groups):
                    half = jnp.where(half_of == g % 2, 0, cols)
                    to = jnp.where(is_own, half + (w - own_lo) // 8 + g // 2, 2 * cols)
                    record[slot, to] = jnp.zeros((4, height, lanes), jnp.float32)
                store_ahead(level, after, 1 - bslot)

            return 1 - bslot

        buf = lax.fori_loop(first, last, block, buf)
        for copy in out_copies(k, slot):
            copy.start()
        return buf

    store_ahead(1 - begin % 2, lo_of(begin) // BLOCK, 0)
    lax.fori_loop(begin, end, one_step, 0)
    for k in (end - 2, end - 1):
        for copy in out_copies(k, (k - begin) % 2):
            copy.wait()


def multiply(keep, got, start, total):
    steps, cols, half, height, lanes = keep.shape
    for c in range(cols):
        for i in range(half):

            def one(k, value, c=c, i=i):
                return value + keep[k, c, i] * got[k, c, i]

            first = start[c, i] if start is not None else jnp.zeros((height, lanes), jnp.float32)
            total[c, i] = lax.fori_loop(0, steps, one, first, unroll=4)


def multiply_kernel(keep, got, total):
    multiply(keep, got, None, total)


def image_kernel(owners, places, before, keep, got, *refs):
    outs, total = refs[:owners], refs[owners]
    per_owner, half, brick_y = outs[0].shape[:3]
    multiply(keep, got, before, total)
    for b in range(owners):
        for rank in range(per_owner):
            m = places[b * per_owner + rank]
            y = pl.multiple_of((m % KY) * brick_y, brick_y)
            for i in range(half):
                outs[b][rank, i] = total[m // KY, i, pl.ds(y, brick_y), :]


def sum_kernel(owners, rows, *refs):
    blocks, out = refs[:-1], refs[-1]
    per_owner = blocks[0].shape[0]
    out[...] = jnp.zeros_like(out)
    for b in range(owners):
        for rank in range(per_owner):
            out[rows[b * per_owner + rank]] += blocks[b][rank]


def call(kernel, out_shape, in_specs, out_specs, scratch=(), mib=8, flops=1):
    return pl.pallas_call(
        kernel,
        out_shape=out_shape,
        in_specs=in_specs,
        out_specs=out_specs,
        scratch_shapes=list(scratch),
        compiler_params=pltpu.CompilerParams(vmem_limit_bytes=mib * MIB),
        cost_estimate=pl.CostEstimate(flops=flops, bytes_accessed=1, transcendentals=0),
    )


def run_steps(sides, span, pulses_of, shape, meta, injects, rims, inputs):
    f32 = jnp.float32
    begin, end, steps = span
    window, height, lanes = shape
    count = len(rims)
    thick = window // count
    cols = thick // 8
    fresh = begin == 0
    kept = jax.ShapeDtypeStruct((end - begin, cols, 4, height, lanes), f32)
    padded = (window + 2 * REACH, height, lanes)
    outs, specs, scratch = [kept, kept], [anywhere, anywhere], []
    if fresh:
        if end < steps:
            outs += [jax.ShapeDtypeStruct((2,) + padded, f32)] + [jax.ShapeDtypeStruct(shape, f32)] * 5
            specs += [vmem] * 6
        else:
            scratch = [pltpu.VMEM((2,) + padded, f32)] + [pltpu.VMEM(shape, f32)] * 5
        scratch += [pltpu.VMEM(padded, f32)]
        in_specs = [vmem] * (2 * count) + [anywhere] * count
    else:
        scratch = [pltpu.VMEM((2,) + padded, f32)]
        in_specs = [vmem] * 6
    return call(
        functools.partial(steps_kernel, sides, span, pulses_of),
        outs,
        [smem, vmem, vmem] + [anywhere] * (len(injects) + count) + in_specs,
        specs,
        scratch
        + [
            pltpu.VMEM((2, window * height, lanes), f32),
            pltpu.VMEM((2, BLOCK * height, 2 * lanes), f32),
            pltpu.VMEM((2, BLOCK // 8, 8 * height, 2 * lanes), f32),
            pltpu.VMEM((2, 2 * cols + 1, 4, height, lanes), f32),
            pltpu.VMEM((end - begin, 2, window, lanes), f32),
            pltpu.SemaphoreType.DMA((2,)),
            pltpu.SemaphoreType.DMA((2, 2)),
            pltpu.SemaphoreType.DMA((count, 3)),
        ],
        mib=12 + window // 4,
        flops=(end - begin) * window * height * lanes * 2048,
    )(meta, z_matrix(lanes), y_matrix(height, 4), *injects, *rims, *inputs)


def injection(window, offset, split, late, height, lanes, is_source, source_cell, receivers, pulses, recorded):
    steps, spots = recorded.shape
    none = jnp.full((spots - 1,), -1, jnp.int32)
    cells = jnp.where(is_source, jnp.concatenate([source_cell, none]), receivers)
    source_values = jnp.concatenate([-pulses[:, None], jnp.zeros((steps, spots - 1), jnp.float32)], axis=1)
    values = jnp.where(is_source, source_values, recorded)
    z = cells % lanes
    rows = cells // lanes - offset * height
    rows = jnp.where(cells >= 0, rows, -1)
    every = lax.broadcasted_iota(jnp.int32, (window * height, spots), 0)
    which_row = (every == rows[None, :]).astype(jnp.bfloat16)
    which_lane = (z[:, None] == lax.broadcasted_iota(jnp.int32, (spots, lanes), 1)).astype(jnp.float32)
    high = lax.reduce_precision(values, 8, 7)
    low = lax.reduce_precision(values - high, 8, 7)
    both = jnp.concatenate([high, low], axis=1)
    spread = both[:, :, None] * jnp.concatenate([which_lane, which_lane], axis=0)[None]
    spread = spread.astype(jnp.bfloat16)
    twice = jnp.concatenate([which_row, which_row], axis=1)

    def product(rows, spread):
        return jnp.einsum("rp,kpz->krz", rows, spread, preferred_element_type=jnp.float32)

    lo, hi = late
    return (
        product(twice, spread[:split]),
        product(twice[lo * height : hi * height], spread[split:]),
    )


def per_device(
    velocity,
    density,
    owner_map,
    footprint,
    aperture,
    source_cell,
    receiver_cells,
    wavelet,
    traces,
    states,
    stored_rims,
):
    f32 = jnp.float32
    owners = lax.axis_size("shot")
    columns = lax.axis_size("dom")
    column = lax.axis_index("dom")
    pair = lax.axis_index("pair")
    shot = lax.axis_index("shot")
    stored, brick_x, brick_y, lanes = velocity.shape
    half_x = brick_x // 2
    slots = footprint.shape[1]
    per_owner = slots // owners
    thick = slots // KY * brick_x
    height = KY * brick_y
    steps = wavelet.shape[1]
    sides = columns == 2
    meta = jnp.stack(
        [shot.astype(jnp.int32), column.astype(jnp.int32), pair.astype(jnp.int32), aperture[0] * brick_x]
    )
    tables = (owner_map.shape[0], slots)

    table = jnp.where(pair == 0, velocity, density)
    prints = [footprint[0]] + [xor_swap(footprint[0], "shot", b) for b in range(1, owners)]
    info = jnp.concatenate([meta, owner_map, *prints])
    split = 13 if sides else 8
    if sides:
        offset = 0
        window = 2 * thick
        late = (0, window)
    else:
        offset = (column - HOPS) * thick
        window = (2 * HOPS + 1) * thick
        deep = REACH * (steps - 1 - split)
        late = (HOPS * thick - deep, (HOPS + 1) * thick + deep)
    early_inject, late_inject = injection(
        window, offset, split, late, height, lanes, pair == 0,
        source_cell, receiver_cells[0], wavelet[0], traces[0],
    )
    brick = jax.ShapeDtypeStruct((per_owner, brick_x, brick_y, lanes), f32)

    fields = slabs_of(states[0, 0])
    listed = jax.ShapeDtypeStruct((slots,), jnp.int32)
    *packed, rows = call(
        functools.partial(pack_kernel, owners, columns, tables),
        [brick] * owners + [listed],
        [smem, anywhere],
        [anywhere] * owners + [smem],
        [pltpu.SemaphoreType.DMA((owners, per_owner))],
    )(info, table)
    got = [packed[0]] + [xor_swap(packed[b], "shot", b) for b in range(1, owners)]
    bricks, places = call(
        functools.partial(unpack_kernel, owners, columns, tables, stored),
        [jax.ShapeDtypeStruct((slots, brick_x, brick_y, lanes), f32), listed],
        [smem] + [vmem] * owners,
        [vmem, smem],
    )(info, *got)
    mine = slabs_of(bricks)
    shape = (window, height, lanes)
    if sides:
        rims_here, _ = lax.optimization_barrier((stored_rims[0], info))
        rim_slabs = slabs_of(rims_here, first_only=True)
        mine[1], early_inject, late_inject, rim_slabs[1] = lax.optimization_barrier(
            (mine[1], early_inject, late_inject, rim_slabs[1])
        )
        theirs = [xor_swap(slab, "pair", 1) for slab in mine]
        keep, send, *carried = run_steps(
            sides, (0, split, steps), [(0, split, 0)], shape, meta, [early_inject], rim_slabs,
            [*mine, *theirs, *fields],
        )
        partner = xor_swap(send, "pair", 1)
        keep_last, send_last = run_steps(
            sides, (split, steps, steps), [(split, steps, 0)], shape, meta, [late_inject], rim_slabs,
            carried,
        )
        total = call(
            multiply_kernel, jax.ShapeDtypeStruct(keep.shape[1:], f32), [vmem] * 2, vmem, mib=16
        )(keep, partner)
    else:
        theirs = [xor_swap(slab, "pair", 1) for slab in mine]
        keep_last, send_last = run_steps(
            sides, (0, steps, steps), [(0, split, 0), (split, steps, late[0] * height)], shape, meta,
            [early_inject, late_inject], slabs_of(stored_rims[0], first_only=True),
            [*mine, *theirs, *fields],
        )
        total = jnp.zeros(keep_last.shape[1:], f32)
    partner_last = xor_swap(send_last, "pair", 1)

    part = jax.ShapeDtypeStruct((per_owner, half_x, brick_y, lanes), f32)
    images = call(
        functools.partial(image_kernel, owners),
        [part] * owners,
        [smem] + [vmem] * 3,
        [vmem] * owners,
        [pltpu.VMEM(total.shape, f32)],
        mib=16,
    )(places, total, keep_last, partner_last)
    returned = [images[0]] + [xor_swap(images[b], "shot", b) for b in range(1, owners)]
    return call(
        functools.partial(sum_kernel, owners),
        jax.ShapeDtypeStruct((stored, half_x, brick_y, lanes), f32),
        [smem] + [vmem] * owners,
        vmem,
    )(rows, *returned)


def solution(mesh):
    placed = (
        P(("groups", "shot", "dom"), None, None, None),
        P(("groups", "shot", "dom"), None, None, None),
        P("groups"),
        P(("groups", "shot"), "dom"),
        P(("groups", "shot")),
        P(("groups", "shot")),
        P(("groups", "shot"), None),
        P(("groups", "shot"), None),
        P(("groups", "shot"), None, None),
        P(("groups", "shot"), "pair", None, "dom", None, None),
        P(("groups", "shot"), None, None, "dom", None),
    )
    return jax.shard_map(
        per_device,
        mesh=mesh,
        in_specs=placed,
        out_specs=P(("groups", "shot", "dom"), "pair", None, None),
        check_vma=False,
    )
```

```python
import functools

import jax
import jax.numpy as jnp
import numpy as np
from jax import lax
from jax.experimental import pallas as pl
from jax.experimental.pallas import tpu as pltpu
from jax.sharding import PartitionSpec as P

KY = 4
REACH = 4

first_weights = (0.8, -0.2, 4.0 / 105.0, -1.0 / 280.0)
second_weights = (-205.0 / 72.0, 1.6, -0.2, 8.0 / 315.0, -1.0 / 560.0)

FIRST = first_weights[2]
SECOND = second_weights[3]
first_ratio = (21.0, -5.25, 1.0, -0.09375)
second_ratio = (63.0, -7.875, 1.0, -0.0703125)

HOPS = 2
META = 4
MIB = 1024 * 1024

smem = pl.BlockSpec(memory_space=pltpu.SMEM)
vmem = pl.BlockSpec(memory_space=pltpu.VMEM)
anywhere = pl.BlockSpec(memory_space=pl.ANY)


def z_matrix(size):
    second = np.zeros((size, size))
    first = np.zeros((size, size))
    for r in range(1, REACH + 1):
        for z in range(size):
            if z + r < size:
                second[z + r, z] = second_ratio[r - 1]
                first[z + r, z] = first_ratio[r - 1]
            if z - r >= 0:
                second[z - r, z] = second_ratio[r - 1]
                first[z - r, z] = -first_ratio[r - 1]
    whole = np.concatenate([second, first], axis=1)
    return np.concatenate([whole, whole], axis=0).astype(jnp.bfloat16)


def y_matrix(across, layers):
    second = np.zeros((across, across))
    first = np.zeros((across, across))
    for r in range(1, REACH + 1):
        for y in range(across):
            if y + r < across:
                second[y, y + r] = second_ratio[r - 1]
                first[y, y + r] = first_ratio[r - 1]
            if y - r >= 0:
                second[y, y - r] = second_ratio[r - 1]
                first[y, y - r] = -first_ratio[r - 1]
    same = np.eye(layers)
    whole = np.concatenate([np.kron(same, second), np.kron(same, first)], axis=0)
    return np.concatenate([whole, whole], axis=1).astype(jnp.bfloat16)


def xor_swap(block, axis, bits):
    size = lax.axis_size(axis)
    return lax.ppermute(block, axis, [(i, i ^ bits) for i in range(size)])


def slabs_of(block, first_only=False):
    size = lax.axis_size("dom")
    pairs = lax.axis_size("pair")

    def shift(x, moves):
        if first_only:
            return lax.ppermute(x, ("dom", "pair"), [(i * pairs, j * pairs) for i, j in moves])
        return lax.ppermute(x, "dom", moves)

    if size == 1:
        return [block]
    if size == 2:
        return [block, shift(block, [(0, 1), (1, 0)])]
    up = [(i, i + 1) for i in range(size - 1)]
    down = [(i + 1, i) for i in range(size - 1)]
    found = [block]
    left = right = block
    for _ in range(HOPS):
        left = shift(left, up)
        right = shift(right, down)
        found = [left] + found + [right]
    return found


def serve(info, bricks, slots, wanted, stored, take):
    def one(m, counts):
        after = []
        for b, (at, base) in enumerate(wanted):
            local = info[META + info[META + bricks + at * slots + m]] - base
            mine = (local >= 0) & (local < stored)

            @pl.when(mine)
            def _(b=b, local=local):
                take(b, m, local, counts[b])

            after.append(counts[b] + mine.astype(jnp.int32))
        return tuple(after)

    lax.fori_loop(0, slots, one, (jnp.int32(0),) * len(wanted))


def pack_kernel(owners, columns, tables, info, table, *refs):
    outs, rows, sems = refs[:owners], refs[owners], refs[owners + 1]
    stored = table.shape[0]
    per_owner = outs[0].shape[0]
    base = (info[0] * columns + info[1]) * stored

    def take(b, m, local, rank):
        rows[b * per_owner + rank] = local
        pltpu.make_async_copy(table.at[local], outs[b].at[rank], sems.at[b, rank]).start()

    serve(info, *tables, [(b, base) for b in range(owners)], stored, take)
    for b, out in enumerate(outs):
        for rank in range(per_owner):
            pltpu.make_async_copy(table.at[0], out.at[rank], sems.at[b, rank]).wait()


def unpack_kernel(owners, columns, tables, stored, info, *refs):
    blocks, out, places = refs[:owners], refs[owners], refs[owners + 1]
    per_owner = blocks[0].shape[0]

    def take(b, m, local, rank):
        places[b * per_owner + rank] = m
        out[m] = blocks[b][rank]

    serve(info, *tables, sources(owners, columns, stored, info), stored, take)


def sources(owners, columns, stored, info):
    return [(0, ((info[0] ^ b) * columns + info[1]) * stored) for b in range(owners)]


def each(f, *lists):
    return [f(*items) for items in zip(*lists)]


def add(a, b):
    return each(lambda p, q: p + q, a, b)


def sub(a, b):
    return each(lambda p, q: p - q, a, b)


def mul(a, b):
    return each(lambda p, q: p * q, a, b)


def scaled(factor, a):
    return [factor * p for p in a]


def along_x(column):
    size = len(column) - 2 * REACH
    lap = slope = None
    for r in (3, 1, 2, 4):
        ahead = column[REACH + r : REACH + r + size]
        behind = column[REACH - r : REACH - r + size]
        total, apart = add(ahead, behind), sub(ahead, behind)
        if r == 3:
            lap, slope = total, apart
        else:
            lap = add(lap, scaled(second_ratio[r - 1], total))
            slope = add(slope, scaled(first_ratio[r - 1], apart))
    return lap, slope


def z_slopes(high, low, zmat):
    both = jnp.concatenate([high, low], axis=1)
    return jnp.dot(both, zmat[...], preferred_element_type=jnp.float32)


def y_slopes(high, low, ymat):
    n = ymat.shape[0] // 2
    both = [
        jnp.concatenate([high[at : at + n], low[at : at + n]], axis=0) for at in range(0, 2 * n, n)
    ]
    return jnp.dot(ymat[...], jnp.concatenate(both, axis=1), preferred_element_type=jnp.float32)


BLOCK = 16


def make_coefficients(
    mine, theirs, places, active, is_source, zmat, ymat, field, logs, square, centre, gx, gy, gz
):
    window, height, lanes = square.shape
    rows8 = height // 8
    zero = jnp.zeros((REACH, height, lanes), jnp.float32)
    for level in range(2):
        field[level, 0:REACH] = zero
        field[level, REACH + window : 2 * REACH + window] = zero
    logs[0:REACH] = zero
    logs[REACH + window : 2 * REACH + window] = zero

    for s in range(len(mine)):

        def fill(m, carry, s=s):
            x0 = places[s] + (m // KY) * 8
            y0 = pl.multiple_of((m % KY) * 8, 8)
            on = active(x0)
            for i in range(8):
                a = mine[s][m, i]
                b = theirs[s][m, i]
                courant = jnp.where(is_source, a, b)
                density = jnp.where(is_source, b, a)
                squared = jnp.where(on, courant * courant, 0.0)
                square[x0 + i, pl.ds(y0, 8), :] = SECOND * squared
                centre[x0 + i, pl.ds(y0, 8), :] = 2.0 + (3.0 * second_weights[0]) * squared
                logs[REACH + x0 + i, pl.ds(y0, 8), :] = jnp.where(
                    on, jnp.log(jnp.where(on, density, 1.0)), 0.0
                )
            return carry

        lax.fori_loop(0, mine[s].shape[0], fill, 0)

    def bend(b, carry):
        w = pl.multiple_of(b * BLOCK, BLOCK)
        value = logs[pl.ds(REACH + w, BLOCK)].reshape(BLOCK * height, lanes)
        high = value.astype(jnp.bfloat16)
        low = (value - high.astype(jnp.float32)).astype(jnp.bfloat16)
        z = z_slopes(high, low, zmat)
        n = 4 * height
        for g in range(BLOCK // 4):
            if g % 2 == 0:
                pair = slice(g * n, g * n + 2 * n)
                y = y_slopes(high[pair], low[pair], ymat)
            side = slice(g % 2 * lanes, g % 2 * lanes + lanes)
            for q in range(rows8):
                part = slice(q * 8, q * 8 + 8)
                _, slope = along_x([logs[w + 4 * g + j, part, :] for j in range(4 + 2 * REACH)])
                for i in range(4):
                    x = w + 4 * g + i
                    at = i * height + q * 8
                    scale = (FIRST * FIRST / SECOND) * square[x, part, :]
                    gx[x, part, :] = scale * slope[i]
                    gy[x, part, :] = scale * y[n + at : n + at + 8, side]
                    gz[x, part, :] = scale * z[g * n + at : g * n + at + 8, lanes:]
        return carry

    lax.fori_loop(0, window // BLOCK, bend, 0, unroll=2)


def steps_kernel(sides, span, pulses_of, meta, zmat, ymat, *refs):
    begin, end, steps = span
    fresh = begin == 0
    count = 2 if sides else 2 * HOPS + 1
    injects, refs = refs[: len(pulses_of)], refs[len(pulses_of) :]
    rims, refs = refs[:count], refs[count:]
    if fresh:
        mine, theirs, refs = refs[:count], refs[count : 2 * count], refs[2 * count :]
        levels, refs = refs[:count], refs[count:]
        keep, send, field, square, centre, gx, gy, gz, logs, *refs = refs
    else:
        carried, square, centre, gx, gy, gz, keep, send, field, *refs = refs
    pulses, zbuf, ybuf, record, rim, sems, out_sems, in_sems = refs
    thick, lanes = rims[0].shape[2:]
    window, height = square.shape[:2]
    cols = thick // 8
    rows8 = height // 8
    column = meta[1]
    is_source = meta[2] == 0
    limit = meta[3]
    half_of = meta[2]
    sublane = lax.broadcasted_iota(jnp.int32, (8, lanes), 0)
    if sides:
        own_lo = column * thick
        places = [column * thick, (1 - column) * thick]
    else:
        own_lo = HOPS * thick
        places = [s * thick for s in range(count)]

    def active(w):
        x = w if sides else w + column * thick - own_lo
        return (x >= 0) & (x < limit)

    def lo_of(k):
        return jnp.maximum(0, own_lo - REACH * (steps - 1 - k))

    def hi_of(k):
        return jnp.minimum(window, own_lo + thick + REACH * (steps - 1 - k))

    def pulse_copies(k, slot, act):
        for inject, (k_lo, k_hi, row_lo) in zip(injects, pulses_of):

            @pl.when((k >= k_lo) & (k < k_hi))
            def _(inject=inject, k_lo=k_lo, row_lo=row_lo):
                there = pulses.at[slot, pl.ds(row_lo, inject.shape[1])]
                act(pltpu.make_async_copy(inject.at[k - k_lo], there, sems.at[slot]))

    def out_copies(k, slot):
        return [
            pltpu.make_async_copy(
                record.at[slot, pl.ds(0, cols)], keep.at[k - begin], out_sems.at[slot, 0]
            ),
            pltpu.make_async_copy(
                record.at[slot, pl.ds(cols, cols)], send.at[k - begin], out_sems.at[slot, 1]
            ),
        ]

    def in_copies(s):
        place = places[s] if isinstance(places[s], int) else pl.multiple_of(places[s], 8)
        copies = [
            pltpu.make_async_copy(
                rims[s].at[pl.ds(begin, end - begin)],
                rim.at[:, :, pl.ds(place, thick), :],
                in_sems.at[s, 2],
            )
        ]
        if fresh:
            copies += [
                pltpu.make_async_copy(
                    levels[s].at[level],
                    field.at[level, pl.ds(REACH + place, thick)],
                    in_sems.at[s, level],
                )
                for level in range(2)
            ]
        return copies

    pulse_copies(begin, 0, lambda copy: copy.start())
    for s in range(count):
        for copy in in_copies(s):
            copy.start()

    if fresh:
        make_coefficients(
            mine, theirs, places, active, is_source, zmat, ymat, field, logs, square, centre, gx, gy, gz
        )
    else:

        def bring(w, carry):
            for level in range(2):
                field[level, w] = carried[level, w]
            return carry

        lax.fori_loop(0, window + 2 * REACH, bring, 0, unroll=4)
    for s in range(count):
        for copy in in_copies(s):
            copy.wait()

    rim_low = (sublane == 0) & is_source
    rim_high = (sublane == 7) & is_source
    groups = BLOCK // 4

    def cut(level, b, at, size):
        w = b * BLOCK + at
        value = field[level, pl.ds(REACH + w, size)].reshape(size * height, lanes)
        high = value.astype(jnp.bfloat16)
        return high, (value - high.astype(jnp.float32)).astype(jnp.bfloat16)

    def store_ahead(level, b, slot):
        high, low = cut(level, b, 0, BLOCK)
        zbuf[slot] = z_slopes(high, low, zmat)
        n = 8 * height
        for h in range(groups // 2):
            pair = slice(h * n, h * n + n)
            ybuf[slot, h] = y_slopes(high[pair], low[pair], ymat)

    def one_step(k, buf):
        old = lax.rem(k, 2)
        new = 1 - old
        slot = lax.rem(k - begin, 2)
        pulse_copies(k, slot, lambda copy: copy.wait())
        pulse_copies(k + 1, 1 - slot, lambda copy: copy.start())

        @pl.when(k >= begin + 2)
        def _():
            for copy in out_copies(k - 2, slot):
                copy.wait()

        first = lo_of(k) // BLOCK
        last = (hi_of(k) + BLOCK - 1) // BLOCK

        first_next = lo_of(k + 1) // BLOCK

        def block(b, bslot):
            w = pl.multiple_of(b * BLOCK, BLOCK)
            on = active(w) | active(w + BLOCK - 8)
            at_end = b == last - 1
            after = jnp.where(at_end, first_next, b + 1)
            level = jnp.where(at_end, old, new)
            is_own = (w >= own_lo) & (w < own_lo + thick)

            @pl.when(on)
            def _():
                top, rest = cut(level, after, 0, BLOCK)
                n = 4 * height
                for g in range(groups):
                    side = slice(g % 2 * lanes, g % 2 * lanes + lanes)
                    half = jnp.where(half_of == g % 2, 0, cols)
                    to = jnp.where(is_own, half + (w - own_lo) // 8 + g // 2, 2 * cols)
                    xs = [w + g * 4 + i for i in range(4)]
                    for q in range(rows8):
                        part = slice(q * 8, q * 8 + 8)
                        column_x = [
                            field[new, w + g * 4 + j, part, :] for j in range(4 + 2 * REACH)
                        ]
                        lap, dx = along_x(column_x)
                        mid = column_x[REACH : REACH + 4]
                        at = [(g * 4 + i) * height + q * 8 for i in range(4)]
                        aty = [i * height + q * 8 for i in range(4)]
                        z2 = [zbuf[bslot, p : p + 8, 0:lanes] for p in at]
                        z1 = [zbuf[bslot, p : p + 8, lanes:] for p in at]
                        y2 = [ybuf[bslot, g // 2, p : p + 8, side] for p in aty]
                        y1 = [ybuf[bslot, g // 2, n + p : n + p + 8, side] for p in aty]
                        lap = add(lap, add(z2, y2))
                        value = sub(
                            mul([centre[x, part, :] for x in xs], mid),
                            [field[old, REACH + x, part, :] for x in xs],
                        )
                        value = add(
                            value,
                            [
                                pulses[slot, pl.ds(pl.multiple_of(x * height + q * 8, 8), 8), :]
                                for x in xs
                            ],
                        )
                        value = add(value, mul([square[x, part, :] for x in xs], lap))
                        drift = mul([gx[x, part, :] for x in xs], dx)
                        drift = add(drift, mul([gy[x, part, :] for x in xs], y1))
                        drift = add(drift, mul([gz[x, part, :] for x in xs], z1))
                        value = sub(value, drift)
                        if q == 0:
                            low = [
                                jnp.broadcast_to(rim[k - begin, 0, pl.ds(x, 1), :], (8, lanes)) for x in xs
                            ]
                            value = each(lambda p, v: jnp.where(rim_low, p, v), low, value)
                        if q == rows8 - 1:
                            high = [
                                jnp.broadcast_to(rim[k - begin, 1, pl.ds(x, 1), :], (8, lanes)) for x in xs
                            ]
                            value = each(lambda p, v: jnp.where(rim_high, p, v), high, value)
                        for i in range(4):
                            field[old, REACH + xs[i], part, :] = value[i]
                            record[slot, to, i, part, :] = value[i]
                zbuf[1 - bslot] = z_slopes(top, rest, zmat)
                for h in range(groups // 2):
                    ybuf[1 - bslot, h] = y_slopes(top[h * 2 * n : h * 2 * n + 2 * n], rest[h * 2 * n : h * 2 * n + 2 * n], ymat)

            for half in range(BLOCK // 8):
                x8 = w + half * 8

                @pl.when(on & jnp.logical_not(active(x8)))
                def _(x8=x8, half=half):
                    field[old, pl.ds(REACH + x8, 8)] = jnp.zeros((8, height, lanes), jnp.float32)
                    for g in range(2):
                        to = jnp.where(is_own, jnp.where(half_of == g, 0, cols) + (x8 - own_lo) // 8, 2 * cols)
                        record[slot, to] = jnp.zeros((4, height, lanes), jnp.float32)

            @pl.when(jnp.logical_not(on))
            def _():
                field[old, pl.ds(REACH + w, BLOCK)] = jnp.zeros((BLOCK, height, lanes), jnp.float32)
                for g in range(groups):
                    half = jnp.where(half_of == g % 2, 0, cols)
                    to = jnp.where(is_own, half + (w - own_lo) // 8 + g // 2, 2 * cols)
                    record[slot, to] = jnp.zeros((4, height, lanes), jnp.float32)
                store_ahead(level, after, 1 - bslot)

            return 1 - bslot

        buf = lax.fori_loop(first, last, block, buf)
        for copy in out_copies(k, slot):
            copy.start()
        return buf

    store_ahead(1 - begin % 2, lo_of(begin) // BLOCK, 0)
    lax.fori_loop(begin, end, one_step, 0)
    for k in (end - 2, end - 1):
        for copy in out_copies(k, (k - begin) % 2):
            copy.wait()


def multiply(keep, got, start, total):
    steps, cols, half, height, lanes = keep.shape
    for c in range(cols):
        for i in range(half):

            def one(k, value, c=c, i=i):
                return value + keep[k, c, i] * got[k, c, i]

            first = start[c, i] if start is not None else jnp.zeros((height, lanes), jnp.float32)
            total[c, i] = lax.fori_loop(0, steps, one, first, unroll=4)


def multiply_kernel(keep, got, total):
    multiply(keep, got, None, total)


def image_kernel(owners, places, before, keep, got, *refs):
    outs, total = refs[:owners], refs[owners]
    per_owner, half, brick_y = outs[0].shape[:3]
    multiply(keep, got, before, total)
    for b in range(owners):
        for rank in range(per_owner):
            m = places[b * per_owner + rank]
            y = pl.multiple_of((m % KY) * brick_y, brick_y)
            for i in range(half):
                outs[b][rank, i] = total[m // KY, i, pl.ds(y, brick_y), :]


def sum_kernel(owners, rows, *refs):
    blocks, out = refs[:-1], refs[-1]
    per_owner = blocks[0].shape[0]
    out[...] = jnp.zeros_like(out)
    for b in range(owners):
        for rank in range(per_owner):
            out[rows[b * per_owner + rank]] += blocks[b][rank]


def call(kernel, out_shape, in_specs, out_specs, scratch=(), mib=8, flops=1):
    return pl.pallas_call(
        kernel,
        out_shape=out_shape,
        in_specs=in_specs,
        out_specs=out_specs,
        scratch_shapes=list(scratch),
        compiler_params=pltpu.CompilerParams(vmem_limit_bytes=mib * MIB),
        cost_estimate=pl.CostEstimate(flops=flops, bytes_accessed=1, transcendentals=0),
    )


def run_steps(sides, span, pulses_of, shape, meta, injects, rims, inputs):
    f32 = jnp.float32
    begin, end, steps = span
    window, height, lanes = shape
    count = len(rims)
    thick = window // count
    cols = thick // 8
    fresh = begin == 0
    kept = jax.ShapeDtypeStruct((end - begin, cols, 4, height, lanes), f32)
    padded = (window + 2 * REACH, height, lanes)
    outs, specs, scratch = [kept, kept], [anywhere, anywhere], []
    if fresh:
        if end < steps:
            outs += [jax.ShapeDtypeStruct((2,) + padded, f32)] + [jax.ShapeDtypeStruct(shape, f32)] * 5
            specs += [vmem] * 6
        else:
            scratch = [pltpu.VMEM((2,) + padded, f32)] + [pltpu.VMEM(shape, f32)] * 5
        scratch += [pltpu.VMEM(padded, f32)]
        in_specs = [vmem] * (2 * count) + [anywhere] * count
    else:
        scratch = [pltpu.VMEM((2,) + padded, f32)]
        in_specs = [vmem] * 6
    return call(
        functools.partial(steps_kernel, sides, span, pulses_of),
        outs,
        [smem, vmem, vmem] + [anywhere] * (len(injects) + count) + in_specs,
        specs,
        scratch
        + [
            pltpu.VMEM((2, window * height, lanes), f32),
            pltpu.VMEM((2, BLOCK * height, 2 * lanes), f32),
            pltpu.VMEM((2, BLOCK // 8, 8 * height, 2 * lanes), f32),
            pltpu.VMEM((2, 2 * cols + 1, 4, height, lanes), f32),
            pltpu.VMEM((end - begin, 2, window, lanes), f32),
            pltpu.SemaphoreType.DMA((2,)),
            pltpu.SemaphoreType.DMA((2, 2)),
            pltpu.SemaphoreType.DMA((count, 3)),
        ],
        mib=12 + window // 4,
        flops=(end - begin) * window * height * lanes * 2048,
    )(meta, z_matrix(lanes), y_matrix(height, 4), *injects, *rims, *inputs)


def injection(window, offset, spans, late, height, lanes, is_source, source_cell, receivers, pulses, recorded):
    steps, spots = recorded.shape
    none = jnp.full((spots - 1,), -1, jnp.int32)
    cells = jnp.where(is_source, jnp.concatenate([source_cell, none]), receivers)
    source_values = jnp.concatenate([-pulses[:, None], jnp.zeros((steps, spots - 1), jnp.float32)], axis=1)
    values = jnp.where(is_source, source_values, recorded)
    z = cells % lanes
    rows = cells // lanes - offset * height
    rows = jnp.where(cells >= 0, rows, -1)
    every = lax.broadcasted_iota(jnp.int32, (window * height, spots), 0)
    which_row = (every == rows[None, :]).astype(jnp.bfloat16)
    which_lane = (z[:, None] == lax.broadcasted_iota(jnp.int32, (spots, lanes), 1)).astype(jnp.float32)
    high = lax.reduce_precision(values, 8, 7)
    low = lax.reduce_precision(values - high, 8, 7)
    both = jnp.concatenate([high, low], axis=1)
    spread = both[:, :, None] * jnp.concatenate([which_lane, which_lane], axis=0)[None]
    spread = spread.astype(jnp.bfloat16)
    twice = jnp.concatenate([which_row, which_row], axis=1)

    def product(rows, spread):
        return jnp.einsum("rp,kpz->krz", rows, spread, preferred_element_type=jnp.float32)

    lo, hi = late
    found = [product(twice, spread[first:last]) for first, last in spans[:-1]]
    first, last = spans[-1]
    return found + [product(twice[lo * height : hi * height], spread[first:last])]


def per_device(
    velocity,
    density,
    owner_map,
    footprint,
    aperture,
    source_cell,
    receiver_cells,
    wavelet,
    traces,
    states,
    stored_rims,
):
    f32 = jnp.float32
    owners = lax.axis_size("shot")
    columns = lax.axis_size("dom")
    column = lax.axis_index("dom")
    pair = lax.axis_index("pair")
    shot = lax.axis_index("shot")
    stored, brick_x, brick_y, lanes = velocity.shape
    half_x = brick_x // 2
    slots = footprint.shape[1]
    per_owner = slots // owners
    thick = slots // KY * brick_x
    height = KY * brick_y
    steps = wavelet.shape[1]
    sides = columns == 2
    meta = jnp.stack(
        [shot.astype(jnp.int32), column.astype(jnp.int32), pair.astype(jnp.int32), aperture[0] * brick_x]
    )
    tables = (owner_map.shape[0], slots)

    table = jnp.where(pair == 0, velocity, density)
    prints = footprint[0]
    for bits in range(owners.bit_length() - 1):
        prints = jnp.concatenate([prints, xor_swap(prints, "shot", 1 << bits)])
    info = jnp.concatenate([meta, owner_map, prints])
    split = 13 if sides else 8
    if sides:
        offset = 0
        window = 2 * thick
        late = (0, window)
    else:
        offset = (column - HOPS) * thick
        window = (2 * HOPS + 1) * thick
        deep = REACH * (steps - 1 - split)
        late = (HOPS * thick - deep, (HOPS + 1) * thick + deep)
    spots, info = lax.optimization_barrier(
        ((source_cell, receiver_cells[0], wavelet[0], traces[0]), info)
    )
    spans = ((0, 3), (3, 13), (13, steps)) if sides else ((0, split), (split, steps))
    injects = injection(window, offset, spans, late, height, lanes, pair == 0, *spots)
    brick = jax.ShapeDtypeStruct((per_owner, brick_x, brick_y, lanes), f32)

    fields = slabs_of(states[0, 0])
    listed = jax.ShapeDtypeStruct((slots,), jnp.int32)
    *packed, rows = call(
        functools.partial(pack_kernel, owners, columns, tables),
        [brick] * owners + [listed],
        [smem, anywhere],
        [anywhere] * owners + [smem],
        [pltpu.SemaphoreType.DMA((owners, per_owner))],
    )(info, table)
    got = [packed[0]] + [xor_swap(packed[b], "shot", b) for b in range(1, owners)]
    if sides:
        got[0], injects[0] = lax.optimization_barrier((got[0], injects[0]))
    bricks, places = call(
        functools.partial(unpack_kernel, owners, columns, tables, stored),
        [jax.ShapeDtypeStruct((slots, brick_x, brick_y, lanes), f32), listed],
        [smem] + [vmem] * owners,
        [vmem, smem],
    )(info, *got)
    mine = slabs_of(bricks)
    shape = (window, height, lanes)
    if sides:
        rims_here, _ = lax.optimization_barrier((stored_rims[0], info))
        rim_slabs = slabs_of(rims_here, first_only=True)
        theirs = [xor_swap(mine[0], "pair", 1)]
        mine[1], injects, rim_slabs[1] = lax.optimization_barrier((mine[1], injects, rim_slabs[1]))
        theirs.append(xor_swap(mine[1], "pair", 1))
        keep, send, *carried = run_steps(
            sides, (0, split, steps), [(*spans[0], 0), (*spans[1], 0)], shape, meta, injects[:2], rim_slabs,
            [*mine, *theirs, *fields],
        )
        partner = xor_swap(send, "pair", 1)
        keep_last, send_last = run_steps(
            sides, (split, steps, steps), [(split, steps, 0)], shape, meta, injects[2:], rim_slabs,
            carried,
        )
        total = call(
            multiply_kernel, jax.ShapeDtypeStruct(keep.shape[1:], f32), [vmem] * 2, vmem, mib=16
        )(keep, partner)
    else:
        theirs = [xor_swap(slab, "pair", 1) for slab in mine]
        keep_last, send_last = run_steps(
            sides, (0, steps, steps), [(0, split, 0), (split, steps, late[0] * height)], shape, meta,
            injects, slabs_of(stored_rims[0], first_only=True),
            [*mine, *theirs, *fields],
        )
        total = jnp.zeros(keep_last.shape[1:], f32)
    partner_last = xor_swap(send_last, "pair", 1)

    part = jax.ShapeDtypeStruct((per_owner, half_x, brick_y, lanes), f32)
    images = call(
        functools.partial(image_kernel, owners),
        [part] * owners,
        [smem] + [vmem] * 3,
        [vmem] * owners,
        [pltpu.VMEM(total.shape, f32)],
        mib=16,
    )(places, total, keep_last, partner_last)
    returned = [images[0]] + [xor_swap(images[b], "shot", b) for b in range(1, owners)]
    return call(
        functools.partial(sum_kernel, owners),
        jax.ShapeDtypeStruct((stored, half_x, brick_y, lanes), f32),
        [smem] + [vmem] * owners,
        vmem,
    )(rows, *returned)


def solution(mesh):
    placed = (
        P(("groups", "shot", "dom"), None, None, None),
        P(("groups", "shot", "dom"), None, None, None),
        P("groups"),
        P(("groups", "shot"), "dom"),
        P(("groups", "shot")),
        P(("groups", "shot")),
        P(("groups", "shot"), None),
        P(("groups", "shot"), None),
        P(("groups", "shot"), None, None),
        P(("groups", "shot"), "pair", None, "dom", None, None),
        P(("groups", "shot"), None, None, "dom", None),
    )
    return jax.shard_map(
        per_device,
        mesh=mesh,
        in_specs=placed,
        out_specs=P(("groups", "shot", "dom"), "pair", None, None),
        check_vma=False,
    )
```

```python
import functools

import jax
import jax.numpy as jnp
import numpy as np
from jax import lax
from jax.experimental import pallas as pl
from jax.experimental.pallas import tpu as pltpu
from jax.sharding import PartitionSpec as P

KY = 4
REACH = 4

first_weights = (0.8, -0.2, 4.0 / 105.0, -1.0 / 280.0)
second_weights = (-205.0 / 72.0, 1.6, -0.2, 8.0 / 315.0, -1.0 / 560.0)

FIRST = first_weights[2]
SECOND = second_weights[3]
first_ratio = (21.0, -5.25, 1.0, -0.09375)
second_ratio = (63.0, -7.875, 1.0, -0.0703125)

HOPS = 2
META = 4
MIB = 1024 * 1024

smem = pl.BlockSpec(memory_space=pltpu.SMEM)
vmem = pl.BlockSpec(memory_space=pltpu.VMEM)
anywhere = pl.BlockSpec(memory_space=pl.ANY)


def z_matrix(size):
    second = np.zeros((size, size))
    first = np.zeros((size, size))
    for r in range(1, REACH + 1):
        for z in range(size):
            if z + r < size:
                second[z + r, z] = second_ratio[r - 1]
                first[z + r, z] = first_ratio[r - 1]
            if z - r >= 0:
                second[z - r, z] = second_ratio[r - 1]
                first[z - r, z] = -first_ratio[r - 1]
    whole = np.concatenate([second, first], axis=1)
    return np.concatenate([whole, whole], axis=0).astype(jnp.bfloat16)


def y_matrix(across, layers):
    second = np.zeros((across, across))
    first = np.zeros((across, across))
    for r in range(1, REACH + 1):
        for y in range(across):
            if y + r < across:
                second[y, y + r] = second_ratio[r - 1]
                first[y, y + r] = first_ratio[r - 1]
            if y - r >= 0:
                second[y, y - r] = second_ratio[r - 1]
                first[y, y - r] = -first_ratio[r - 1]
    same = np.eye(layers)
    whole = np.concatenate([np.kron(same, second), np.kron(same, first)], axis=0)
    return np.concatenate([whole, whole], axis=1).astype(jnp.bfloat16)


def xor_swap(block, axis, bits):
    size = lax.axis_size(axis)
    return lax.ppermute(block, axis, [(i, i ^ bits) for i in range(size)])


def slabs_of(block, first_only=False):
    size = lax.axis_size("dom")
    pairs = lax.axis_size("pair")

    def shift(x, moves):
        if first_only:
            return lax.ppermute(x, ("dom", "pair"), [(i * pairs, j * pairs) for i, j in moves])
        return lax.ppermute(x, "dom", moves)

    if size == 1:
        return [block]
    if size == 2:
        return [block, shift(block, [(0, 1), (1, 0)])]
    up = [(i, i + 1) for i in range(size - 1)]
    down = [(i + 1, i) for i in range(size - 1)]
    found = [block]
    left = right = block
    for _ in range(HOPS):
        left = shift(left, up)
        right = shift(right, down)
        found = [left] + found + [right]
    return found


def serve(info, bricks, slots, wanted, stored, take):
    def one(m, counts):
        after = []
        for b, (at, base) in enumerate(wanted):
            local = info[META + info[META + bricks + at * slots + m]] - base
            mine = (local >= 0) & (local < stored)

            @pl.when(mine)
            def _(b=b, local=local):
                take(b, m, local, counts[b])

            after.append(counts[b] + mine.astype(jnp.int32))
        return tuple(after)

    lax.fori_loop(0, slots, one, (jnp.int32(0),) * len(wanted))


def pack_kernel(owners, columns, tables, info, table, *refs):
    outs, rows, sems = refs[:owners], refs[owners], refs[owners + 1]
    stored = table.shape[0]
    per_owner = outs[0].shape[0]
    base = (info[0] * columns + info[1]) * stored

    def take(b, m, local, rank):
        rows[b * per_owner + rank] = local
        pltpu.make_async_copy(table.at[local], outs[b].at[rank], sems.at[b, rank]).start()

    serve(info, *tables, [(b, base) for b in range(owners)], stored, take)
    for b, out in enumerate(outs):
        for rank in range(per_owner):
            pltpu.make_async_copy(table.at[0], out.at[rank], sems.at[b, rank]).wait()


def unpack_kernel(owners, columns, tables, stored, info, *refs):
    blocks, out, places = refs[:owners], refs[owners], refs[owners + 1]
    per_owner = blocks[0].shape[0]

    def take(b, m, local, rank):
        places[b * per_owner + rank] = m
        out[m] = blocks[b][rank]

    serve(info, *tables, sources(owners, columns, stored, info), stored, take)


def sources(owners, columns, stored, info):
    return [(0, ((info[0] ^ b) * columns + info[1]) * stored) for b in range(owners)]


def each(f, *lists):
    return [f(*items) for items in zip(*lists)]


def add(a, b):
    return each(lambda p, q: p + q, a, b)


def sub(a, b):
    return each(lambda p, q: p - q, a, b)


def mul(a, b):
    return each(lambda p, q: p * q, a, b)


def scaled(factor, a):
    return [factor * p for p in a]


def along_x(column):
    size = len(column) - 2 * REACH
    lap = slope = None
    for r in (3, 1, 2, 4):
        ahead = column[REACH + r : REACH + r + size]
        behind = column[REACH - r : REACH - r + size]
        total, apart = add(ahead, behind), sub(ahead, behind)
        if r == 3:
            lap, slope = total, apart
        else:
            lap = add(lap, scaled(second_ratio[r - 1], total))
            slope = add(slope, scaled(first_ratio[r - 1], apart))
    return lap, slope


def z_slopes(high, low, zmat):
    both = jnp.concatenate([high, low], axis=1)
    return jnp.dot(both, zmat[...], preferred_element_type=jnp.float32)


def y_slopes(high, low, ymat):
    n = ymat.shape[0] // 2
    both = [
        jnp.concatenate([high[at : at + n], low[at : at + n]], axis=0) for at in range(0, 2 * n, n)
    ]
    return jnp.dot(ymat[...], jnp.concatenate(both, axis=1), preferred_element_type=jnp.float32)


BLOCK = 16


def make_coefficients(
    mine, theirs, places, active, is_source, zmat, ymat, field, logs, square, centre, gx, gy, gz
):
    window, height, lanes = square.shape
    rows8 = height // 8
    zero = jnp.zeros((REACH, height, lanes), jnp.float32)
    for level in range(2):
        field[level, 0:REACH] = zero
        field[level, REACH + window : 2 * REACH + window] = zero
    logs[0:REACH] = zero
    logs[REACH + window : 2 * REACH + window] = zero

    for s in range(len(mine)):

        def fill(m, carry, s=s):
            x0 = places[s] + (m // KY) * 8
            y0 = pl.multiple_of((m % KY) * 8, 8)
            on = active(x0)
            for i in range(8):
                a = mine[s][m, i]
                b = theirs[s][m, i]
                courant = jnp.where(is_source, a, b)
                density = jnp.where(is_source, b, a)
                squared = jnp.where(on, courant * courant, 0.0)
                square[x0 + i, pl.ds(y0, 8), :] = SECOND * squared
                centre[x0 + i, pl.ds(y0, 8), :] = 2.0 + (3.0 * second_weights[0]) * squared
                logs[REACH + x0 + i, pl.ds(y0, 8), :] = jnp.where(
                    on, jnp.log(jnp.where(on, density, 1.0)), 0.0
                )
            return carry

        lax.fori_loop(0, mine[s].shape[0], fill, 0, unroll=2)

    def bend(b, carry):
        w = pl.multiple_of(b * BLOCK, BLOCK)
        value = logs[pl.ds(REACH + w, BLOCK)].reshape(BLOCK * height, lanes)
        high = value.astype(jnp.bfloat16)
        low = (value - high.astype(jnp.float32)).astype(jnp.bfloat16)
        z = z_slopes(high, low, zmat)
        n = 4 * height
        for g in range(BLOCK // 4):
            if g % 2 == 0:
                pair = slice(g * n, g * n + 2 * n)
                y = y_slopes(high[pair], low[pair], ymat)
            side = slice(g % 2 * lanes, g % 2 * lanes + lanes)
            for q in range(rows8):
                part = slice(q * 8, q * 8 + 8)
                _, slope = along_x([logs[w + 4 * g + j, part, :] for j in range(4 + 2 * REACH)])
                for i in range(4):
                    x = w + 4 * g + i
                    at = i * height + q * 8
                    scale = (FIRST * FIRST / SECOND) * square[x, part, :]
                    gx[x, part, :] = scale * slope[i]
                    gy[x, part, :] = scale * y[n + at : n + at + 8, side]
                    gz[x, part, :] = scale * z[g * n + at : g * n + at + 8, lanes:]
        return carry

    lax.fori_loop(0, window // BLOCK, bend, 0, unroll=2 if window // BLOCK % 4 else 4)


def steps_kernel(sides, span, pulses_of, meta, zmat, ymat, *refs):
    begin, end, steps = span
    fresh = begin == 0
    count = 2 if sides else 2 * HOPS + 1
    injects, refs = refs[: len(pulses_of)], refs[len(pulses_of) :]
    rims, refs = refs[:count], refs[count:]
    if fresh:
        mine, theirs, refs = refs[:count], refs[count : 2 * count], refs[2 * count :]
        levels, refs = refs[:count], refs[count:]
        keep, send, field, square, centre, gx, gy, gz, logs, *refs = refs
    else:
        carried, square, centre, gx, gy, gz, keep, send, field, *refs = refs
    pulses, zbuf, ybuf, record, rim, sems, out_sems, in_sems = refs
    thick, lanes = rims[0].shape[2:]
    window, height = square.shape[:2]
    cols = thick // 8
    rows8 = height // 8
    column = meta[1]
    is_source = meta[2] == 0
    limit = meta[3]
    half_of = meta[2]
    sublane = lax.broadcasted_iota(jnp.int32, (8, lanes), 0)
    if sides:
        own_lo = column * thick
        places = [column * thick, (1 - column) * thick]
    else:
        own_lo = HOPS * thick
        places = [s * thick for s in range(count)]

    def active(w):
        x = w if sides else w + column * thick - own_lo
        return (x >= 0) & (x < limit)

    def lo_of(k):
        return jnp.maximum(0, own_lo - REACH * (steps - 1 - k))

    def hi_of(k):
        return jnp.minimum(window, own_lo + thick + REACH * (steps - 1 - k))

    def pulse_copies(k, slot, act):
        for inject, (k_lo, k_hi, row_lo) in zip(injects, pulses_of):

            @pl.when((k >= k_lo) & (k < k_hi))
            def _(inject=inject, k_lo=k_lo, row_lo=row_lo):
                there = pulses.at[slot, pl.ds(row_lo, inject.shape[1])]
                act(pltpu.make_async_copy(inject.at[k - k_lo], there, sems.at[slot]))

    def out_copies(k, slot):
        return [
            pltpu.make_async_copy(
                record.at[slot, pl.ds(0, cols)], keep.at[k - begin], out_sems.at[slot, 0]
            ),
            pltpu.make_async_copy(
                record.at[slot, pl.ds(cols, cols)], send.at[k - begin], out_sems.at[slot, 1]
            ),
        ]

    def in_copies(s):
        place = places[s] if isinstance(places[s], int) else pl.multiple_of(places[s], 8)
        copies = [
            pltpu.make_async_copy(
                rims[s].at[pl.ds(begin, end - begin)],
                rim.at[:, :, pl.ds(place, thick), :],
                in_sems.at[s, 2],
            )
        ]
        if fresh:
            copies += [
                pltpu.make_async_copy(
                    levels[s].at[level],
                    field.at[level, pl.ds(REACH + place, thick)],
                    in_sems.at[s, level],
                )
                for level in range(2)
            ]
        return copies

    pulse_copies(begin, 0, lambda copy: copy.start())
    for s in range(count):
        for copy in in_copies(s):
            copy.start()

    if fresh:
        make_coefficients(
            mine, theirs, places, active, is_source, zmat, ymat, field, logs, square, centre, gx, gy, gz
        )
    else:

        def bring(w, carry):
            for level in range(2):
                field[level, w] = carried[level, w]
            return carry

        lax.fori_loop(0, window + 2 * REACH, bring, 0, unroll=4)

    rim_low = (sublane == 0) & is_source
    rim_high = (sublane == 7) & is_source
    groups = BLOCK // 4

    def cut(level, b, at, size):
        w = b * BLOCK + at
        value = field[level, pl.ds(REACH + w, size)].reshape(size * height, lanes)
        high = value.astype(jnp.bfloat16)
        return high, (value - high.astype(jnp.float32)).astype(jnp.bfloat16)

    def store_ahead(level, b, slot):
        high, low = cut(level, b, 0, BLOCK)
        zbuf[slot] = z_slopes(high, low, zmat)
        n = 8 * height
        for h in range(groups // 2):
            pair = slice(h * n, h * n + n)
            ybuf[slot, h] = y_slopes(high[pair], low[pair], ymat)

    def one_step(k, buf):
        old = lax.rem(k, 2)
        new = 1 - old
        slot = lax.rem(k - begin, 2)
        pulse_copies(k, slot, lambda copy: copy.wait())
        pulse_copies(k + 1, 1 - slot, lambda copy: copy.start())

        @pl.when(k >= begin + 2)
        def _():
            for copy in out_copies(k - 2, slot):
                copy.wait()

        first = lo_of(k) // BLOCK
        last = (hi_of(k) + BLOCK - 1) // BLOCK

        first_next = lo_of(k + 1) // BLOCK

        def block(b, bslot):
            w = pl.multiple_of(b * BLOCK, BLOCK)
            on = active(w) | active(w + BLOCK - 8)
            at_end = b == last - 1
            after = jnp.where(at_end, first_next, b + 1)
            level = jnp.where(at_end, old, new)
            is_own = (w >= own_lo) & (w < own_lo + thick)

            @pl.when(on)
            def _():
                top, rest = cut(level, after, 0, BLOCK)
                n = 4 * height
                for g in range(groups):
                    side = slice(g % 2 * lanes, g % 2 * lanes + lanes)
                    half = jnp.where(half_of == g % 2, 0, cols)
                    to = jnp.where(is_own, half + (w - own_lo) // 8 + g // 2, 2 * cols)
                    xs = [w + g * 4 + i for i in range(4)]
                    for q in range(rows8):
                        part = slice(q * 8, q * 8 + 8)
                        column_x = [
                            field[new, w + g * 4 + j, part, :] for j in range(4 + 2 * REACH)
                        ]
                        lap, dx = along_x(column_x)
                        mid = column_x[REACH : REACH + 4]
                        at = [(g * 4 + i) * height + q * 8 for i in range(4)]
                        aty = [i * height + q * 8 for i in range(4)]
                        z2 = [zbuf[bslot, p : p + 8, 0:lanes] for p in at]
                        z1 = [zbuf[bslot, p : p + 8, lanes:] for p in at]
                        y2 = [ybuf[bslot, g // 2, p : p + 8, side] for p in aty]
                        y1 = [ybuf[bslot, g // 2, n + p : n + p + 8, side] for p in aty]
                        lap = add(lap, add(z2, y2))
                        value = sub(
                            mul([centre[x, part, :] for x in xs], mid),
                            [field[old, REACH + x, part, :] for x in xs],
                        )
                        value = add(
                            value,
                            [
                                pulses[slot, pl.ds(pl.multiple_of(x * height + q * 8, 8), 8), :]
                                for x in xs
                            ],
                        )
                        value = add(value, mul([square[x, part, :] for x in xs], lap))
                        drift = mul([gy[x, part, :] for x in xs], y1)
                        drift = add(drift, mul([gz[x, part, :] for x in xs], z1))
                        drift = add(drift, mul([gx[x, part, :] for x in xs], dx))
                        value = sub(value, drift)
                        if q == 0:
                            low = [
                                jnp.broadcast_to(rim[k - begin, 0, pl.ds(x, 1), :], (8, lanes)) for x in xs
                            ]
                            value = each(lambda p, v: jnp.where(rim_low, p, v), low, value)
                        if q == rows8 - 1:
                            high = [
                                jnp.broadcast_to(rim[k - begin, 1, pl.ds(x, 1), :], (8, lanes)) for x in xs
                            ]
                            value = each(lambda p, v: jnp.where(rim_high, p, v), high, value)
                        for i in range(4):
                            field[old, REACH + xs[i], part, :] = value[i]
                            record[slot, to, i, part, :] = value[i]
                zbuf[1 - bslot] = z_slopes(top, rest, zmat)
                for h in range(groups // 2):
                    ybuf[1 - bslot, h] = y_slopes(top[h * 2 * n : h * 2 * n + 2 * n], rest[h * 2 * n : h * 2 * n + 2 * n], ymat)

            for half in range(BLOCK // 8):
                x8 = w + half * 8

                @pl.when(on & jnp.logical_not(active(x8)))
                def _(x8=x8, half=half):
                    field[old, pl.ds(REACH + x8, 8)] = jnp.zeros((8, height, lanes), jnp.float32)
                    for g in range(2):
                        to = jnp.where(is_own, jnp.where(half_of == g, 0, cols) + (x8 - own_lo) // 8, 2 * cols)
                        record[slot, to] = jnp.zeros((4, height, lanes), jnp.float32)

            @pl.when(jnp.logical_not(on))
            def _():
                field[old, pl.ds(REACH + w, BLOCK)] = jnp.zeros((BLOCK, height, lanes), jnp.float32)
                for g in range(groups):
                    half = jnp.where(half_of == g % 2, 0, cols)
                    to = jnp.where(is_own, half + (w - own_lo) // 8 + g // 2, 2 * cols)
                    record[slot, to] = jnp.zeros((4, height, lanes), jnp.float32)
                store_ahead(level, after, 1 - bslot)

            return 1 - bslot

        buf = lax.fori_loop(first, last, block, buf)
        for copy in out_copies(k, slot):
            copy.start()
        return buf

    for s in range(count):
        for copy in in_copies(s)[1:]:
            copy.wait()
    store_ahead(1 - begin % 2, lo_of(begin) // BLOCK, 0)
    for s in range(count):
        in_copies(s)[0].wait()
    lax.fori_loop(begin, end, one_step, 0)
    for k in (end - 2, end - 1):
        for copy in out_copies(k, (k - begin) % 2):
            copy.wait()


def multiply(keep, got, start, total):
    steps, cols, half, height, lanes = keep.shape
    for c in range(cols):
        for i in range(half):

            def one(k, value, c=c, i=i):
                return value + keep[k, c, i] * got[k, c, i]

            first = start[c, i] if start is not None else jnp.zeros((height, lanes), jnp.float32)
            total[c, i] = lax.fori_loop(0, steps, one, first, unroll=4)


def multiply_kernel(keep, got, total):
    multiply(keep, got, None, total)


def image_kernel(owners, places, before, keep, got, *refs):
    outs, total = refs[:owners], refs[owners]
    per_owner, half, brick_y = outs[0].shape[:3]
    multiply(keep, got, before, total)
    for b in range(owners):
        for rank in range(per_owner):
            m = places[b * per_owner + rank]
            y = pl.multiple_of((m % KY) * brick_y, brick_y)
            for i in range(half):
                outs[b][rank, i] = total[m // KY, i, pl.ds(y, brick_y), :]


def sum_kernel(owners, rows, *refs):
    blocks, out = refs[:-1], refs[-1]
    per_owner = blocks[0].shape[0]
    out[...] = jnp.zeros_like(out)
    for b in range(owners):
        for rank in range(per_owner):
            out[rows[b * per_owner + rank]] += blocks[b][rank]


def call(kernel, out_shape, in_specs, out_specs, scratch=(), mib=8, flops=1):
    return pl.pallas_call(
        kernel,
        out_shape=out_shape,
        in_specs=in_specs,
        out_specs=out_specs,
        scratch_shapes=list(scratch),
        compiler_params=pltpu.CompilerParams(vmem_limit_bytes=mib * MIB),
        cost_estimate=pl.CostEstimate(flops=flops, bytes_accessed=1, transcendentals=0),
    )


def run_steps(sides, span, pulses_of, shape, meta, injects, rims, inputs):
    f32 = jnp.float32
    begin, end, steps = span
    window, height, lanes = shape
    count = len(rims)
    thick = window // count
    cols = thick // 8
    fresh = begin == 0
    kept = jax.ShapeDtypeStruct((end - begin, cols, 4, height, lanes), f32)
    padded = (window + 2 * REACH, height, lanes)
    outs, specs, scratch = [kept, kept], [anywhere, anywhere], []
    if fresh:
        if end < steps:
            outs += [jax.ShapeDtypeStruct((2,) + padded, f32)] + [jax.ShapeDtypeStruct(shape, f32)] * 5
            specs += [vmem] * 6
        else:
            scratch = [pltpu.VMEM((2,) + padded, f32)] + [pltpu.VMEM(shape, f32)] * 5
        scratch += [pltpu.VMEM(padded, f32)]
        in_specs = [vmem] * (2 * count) + [anywhere] * count
    else:
        scratch = [pltpu.VMEM((2,) + padded, f32)]
        in_specs = [vmem] * 6
    return call(
        functools.partial(steps_kernel, sides, span, pulses_of),
        outs,
        [smem, vmem, vmem] + [anywhere] * (len(injects) + count) + in_specs,
        specs,
        scratch
        + [
            pltpu.VMEM((2, window * height, lanes), f32),
            pltpu.VMEM((2, BLOCK * height, 2 * lanes), f32),
            pltpu.VMEM((2, BLOCK // 8, 8 * height, 2 * lanes), f32),
            pltpu.VMEM((2, 2 * cols + 1, 4, height, lanes), f32),
            pltpu.VMEM((end - begin, 2, window, lanes), f32),
            pltpu.SemaphoreType.DMA((2,)),
            pltpu.SemaphoreType.DMA((2, 2)),
            pltpu.SemaphoreType.DMA((count, 3)),
        ],
        mib=12 + window // 4,
        flops=(end - begin) * window * height * lanes * 2048,
    )(meta, z_matrix(lanes), y_matrix(height, 4), *injects, *rims, *inputs)


def injection(window, offset, spans, late, height, lanes, is_source, source_cell, receivers, pulses, recorded):
    steps, spots = recorded.shape
    none = jnp.full((spots - 1,), -1, jnp.int32)
    cells = jnp.where(is_source, jnp.concatenate([source_cell, none]), receivers)
    source_values = jnp.concatenate([-pulses[:, None], jnp.zeros((steps, spots - 1), jnp.float32)], axis=1)
    values = jnp.where(is_source, source_values, recorded)
    z = cells % lanes
    rows = cells // lanes - offset * height
    rows = jnp.where(cells >= 0, rows, -1)
    every = lax.broadcasted_iota(jnp.int32, (window * height, spots), 0)
    which_row = (every == rows[None, :]).astype(jnp.bfloat16)
    which_lane = (z[:, None] == lax.broadcasted_iota(jnp.int32, (spots, lanes), 1)).astype(jnp.float32)
    high = lax.reduce_precision(values, 8, 7)
    low = lax.reduce_precision(values - high, 8, 7)
    both = jnp.concatenate([high, low], axis=1)
    spread = both[:, :, None] * jnp.concatenate([which_lane, which_lane], axis=0)[None]
    spread = spread.astype(jnp.bfloat16)
    twice = jnp.concatenate([which_row, which_row], axis=1)

    def product(rows, spread):
        return jnp.einsum("rp,kpz->krz", rows, spread, preferred_element_type=jnp.float32)

    lo, hi = late
    found = [product(twice, spread[first:last]) for first, last in spans[:-1]]
    first, last = spans[-1]
    return found + [product(twice[lo * height : hi * height], spread[first:last])]


def per_device(
    velocity,
    density,
    owner_map,
    footprint,
    aperture,
    source_cell,
    receiver_cells,
    wavelet,
    traces,
    states,
    stored_rims,
):
    f32 = jnp.float32
    owners = lax.axis_size("shot")
    columns = lax.axis_size("dom")
    column = lax.axis_index("dom")
    pair = lax.axis_index("pair")
    shot = lax.axis_index("shot")
    stored, brick_x, brick_y, lanes = velocity.shape
    half_x = brick_x // 2
    slots = footprint.shape[1]
    per_owner = slots // owners
    thick = slots // KY * brick_x
    height = KY * brick_y
    steps = wavelet.shape[1]
    sides = columns == 2
    meta = jnp.stack(
        [shot.astype(jnp.int32), column.astype(jnp.int32), pair.astype(jnp.int32), aperture[0] * brick_x]
    )
    tables = (owner_map.shape[0], slots)

    table = jnp.where(pair == 0, velocity, density)
    prints = footprint[0]
    for bits in range(owners.bit_length() - 1):
        prints = jnp.concatenate([prints, xor_swap(prints, "shot", 1 << bits)])
    info = jnp.concatenate([meta, owner_map, prints])
    split = 13 if sides else 8
    if sides:
        offset = 0
        window = 2 * thick
        late = (0, window)
    else:
        offset = (column - HOPS) * thick
        window = (2 * HOPS + 1) * thick
        deep = REACH * (steps - 1 - split)
        late = (HOPS * thick - deep, (HOPS + 1) * thick + deep)
    spots, info = lax.optimization_barrier(
        ((source_cell, receiver_cells[0], wavelet[0], traces[0]), info)
    )
    spans = ((0, 3), (3, 13), (13, steps)) if sides else ((0, split), (split, steps))
    injects = injection(window, offset, spans, late, height, lanes, pair == 0, *spots)
    brick = jax.ShapeDtypeStruct((per_owner, brick_x, brick_y, lanes), f32)

    fields = slabs_of(states[0, 0])
    listed = jax.ShapeDtypeStruct((slots,), jnp.int32)
    *packed, rows = call(
        functools.partial(pack_kernel, owners, columns, tables),
        [brick] * owners + [listed],
        [smem, anywhere],
        [anywhere] * owners + [smem],
        [pltpu.SemaphoreType.DMA((owners, per_owner))],
    )(info, table)
    got = [packed[0]] + [xor_swap(packed[b], "shot", b) for b in range(1, owners)]
    if sides:
        got[0], injects[0] = lax.optimization_barrier((got[0], injects[0]))
    bricks, places = call(
        functools.partial(unpack_kernel, owners, columns, tables, stored),
        [jax.ShapeDtypeStruct((slots, brick_x, brick_y, lanes), f32), listed],
        [smem] + [vmem] * owners,
        [vmem, smem],
    )(info, *got)
    mine = slabs_of(bricks)
    shape = (window, height, lanes)
    if sides:
        rims_here, _ = lax.optimization_barrier((stored_rims[0], info))
        rim_slabs = slabs_of(rims_here, first_only=True)
        theirs = [xor_swap(mine[0], "pair", 1)]
        mine[1], injects, rim_slabs[1] = lax.optimization_barrier((mine[1], injects, rim_slabs[1]))
        theirs.append(xor_swap(mine[1], "pair", 1))
        keep, send, *carried = run_steps(
            sides, (0, split, steps), [(*spans[0], 0), (*spans[1], 0)], shape, meta, injects[:2], rim_slabs,
            [*mine, *theirs, *fields],
        )
        partner = xor_swap(send, "pair", 1)
        keep_last, send_last = run_steps(
            sides, (split, steps, steps), [(split, steps, 0)], shape, meta, injects[2:], rim_slabs,
            carried,
        )
        total = call(
            multiply_kernel, jax.ShapeDtypeStruct(keep.shape[1:], f32), [vmem] * 2, vmem, mib=16
        )(keep, partner)
    else:
        theirs = [xor_swap(slab, "pair", 1) for slab in mine]
        keep_last, send_last = run_steps(
            sides, (0, steps, steps), [(0, split, 0), (split, steps, late[0] * height)], shape, meta,
            injects, slabs_of(stored_rims[0], first_only=True),
            [*mine, *theirs, *fields],
        )
        total = jnp.zeros(keep_last.shape[1:], f32)
    partner_last = xor_swap(send_last, "pair", 1)

    part = jax.ShapeDtypeStruct((per_owner, half_x, brick_y, lanes), f32)
    images = call(
        functools.partial(image_kernel, owners),
        [part] * owners,
        [smem] + [vmem] * 3,
        [vmem] * owners,
        [pltpu.VMEM(total.shape, f32)],
        mib=16,
    )(places, total, keep_last, partner_last)
    returned = [images[0]] + [xor_swap(images[b], "shot", b) for b in range(1, owners)]
    return call(
        functools.partial(sum_kernel, owners),
        jax.ShapeDtypeStruct((stored, half_x, brick_y, lanes), f32),
        [smem] + [vmem] * owners,
        vmem,
    )(rows, *returned)


def solution(mesh):
    placed = (
        P(("groups", "shot", "dom"), None, None, None),
        P(("groups", "shot", "dom"), None, None, None),
        P("groups"),
        P(("groups", "shot"), "dom"),
        P(("groups", "shot")),
        P(("groups", "shot")),
        P(("groups", "shot"), None),
        P(("groups", "shot"), None),
        P(("groups", "shot"), None, None),
        P(("groups", "shot"), "pair", None, "dom", None, None),
        P(("groups", "shot"), None, None, "dom", None),
    )
    return jax.shard_map(
        per_device,
        mesh=mesh,
        in_specs=placed,
        out_specs=P(("groups", "shot", "dom"), "pair", None, None),
        check_vma=False,
    )
```
